128 devices in a mesh: dp: 16 (over y_hi, x, core), tensor: 4 (over z), proj: 2 (over y_lo).
Axes of the slice: x: 4, y: 4 (y_hi: 2, y_lo: 2; y = y_hi * 2 + y_lo), z: 4, core: 2. Of those that a mesh axis runs over, the one named last changes fastest.
Arguments:
- acts: bfloat16 [160, 1024, 4096], P(('dp', 'proj'), None, 'tensor'), may hold values from -6 to 6
- cotangent: bfloat16 [160, 1024, 4096], P(('dp', 'proj'), None, 'tensor'), may hold values from -6 to 6
- adapter_down: bfloat16 [4096, 128], P('tensor'), may hold values from -0.09375 to 0.09375
- adapter_up: bfloat16 [128, 4096], P(None, 'tensor'), may hold values from -0.09375 to 0.09375
- lengths: int32 [160], P(('dp', 'proj')), may hold values from 256 to 1024, as said below
- projection_rows: int32 [4, 32, 64], P('tensor', ('dp', 'proj')), may hold values from 0 to 31
- projection_blocks: bfloat16 [4, 32, 64, 256, 128], P('tensor', ('dp', 'proj')), may hold values from -1 to 1
Outputs:
- features: float32 [160, 8192], P(('dp', 'proj'), 'tensor')
The draws below stay inside these ranges and needn't reach their ends.
Inputs may be any that keep to these rules, and one draw needn't show every extreme that they name: `lengths`: every sequence has at least 256 tokens; some sequence has exactly 1024.
All inputs are finite; a program needn't handle non-finite values.
Results may differ from the reference program's by a relative error of at most 0.0041.
Values may be sent and summed in bfloat16 or wider, within the bound.
A program may use at most 128 MiB of HBM per device.

```python
import jax
import jax.numpy as jnp
from jax import lax

MODEL_WIDTH = 4096
ADAPTER_RANK = 128
OB = 128
LEN = 1024
SEQS = 160
NB_OUT = 64
WPARTS = 4
RPARTS = 32
ROWS = 32


def draw_lengths(key, part):
    base = jax.random.randint(key, (SEQS,), LEN // 4, LEN + 1, dtype=jnp.int32)
    longest = jax.random.randint(jax.random.fold_in(key, 7), (), 0, SEQS, dtype=jnp.int32)
    return jnp.where(jnp.arange(SEQS, dtype=jnp.int32) == longest, jnp.int32(LEN), base)


def set_ends(values, own_key, least, largest):
    shape = values.shape
    index_at = [jax.random.randint(jax.random.fold_in(own_key, axis), (), 0, shape[axis]) for axis in range(len(shape))]
    values = values.at[tuple(index_at)].set(least)
    longest = shape.index(max(shape))
    index_at[longest] = (index_at[longest] + 1) % shape[longest]
    return values.at[tuple(index_at)].set(largest)


def shard_levels(rng, extent, shards, least, largest):
    def one(axis_at, blocks):
        draws = jax.random.uniform(jax.random.fold_in(jax.random.fold_in(rng, 6), axis_at), (blocks,), jnp.float32, least / len(shards), largest / len(shards))
        return jnp.repeat(jnp.exp(draws), extent[axis_at] // blocks).reshape((-1,) + (1,) * (len(extent) - axis_at - 1))

    gain = one(*shards[0])
    for cut in shards[1:]:
        gain = gain * one(*cut)
    return gain


def scatter_about(key, extent, width, most, split=(), held_as=jnp.bfloat16):
    array = width * jax.random.normal(key, extent, jnp.float32)
    if split:
        array = array * shard_levels(key, extent, split, -0.22, 0.18)
    return jnp.clip(array, -most, most).astype(held_as)


def setup_inputs(seed: int = 0) -> dict:
    key_list = jax.random.split(jax.random.key(seed), 8)
    return {
        "acts": scatter_about(key_list[0], (SEQS, LEN, MODEL_WIDTH), 1.0, 6.0, ((0, 32), (2, 4))),
        "cotangent": scatter_about(key_list[1], (SEQS, LEN, MODEL_WIDTH), 1.0, 6.0, ((0, 32), (2, 4))),
        "adapter_down": scatter_about(key_list[2], (MODEL_WIDTH, ADAPTER_RANK), MODEL_WIDTH ** -0.5, 0.09375, ((0, 4),)),
        "adapter_up": scatter_about(key_list[3], (ADAPTER_RANK, MODEL_WIDTH), MODEL_WIDTH ** -0.5, 0.09375, ((1, 4),)),
        "lengths": draw_lengths(jax.random.fold_in(key_list[7], 71), 0),
        "projection_rows": set_ends(jax.random.randint(key_list[5], (WPARTS, RPARTS, NB_OUT), 0, ROWS), jax.random.fold_in(key_list[5], 1), 0, ROWS - 1).astype(jnp.int32),
        "projection_blocks": scatter_about(key_list[6], (WPARTS, RPARTS, NB_OUT, 2 * ADAPTER_RANK, OB), (2 * ADAPTER_RANK * WPARTS * RPARTS // LEN) ** -0.5, 1.0, ((0, 4), (1, 32))),
    }


def reference(acts, cotangent, adapter_down, adapter_up, lengths, projection_rows, projection_blocks):
    positions = jnp.arange(LEN, dtype=jnp.int32)

    def one_sequence(inputs_one):
        sequence_activations, sequence_cotangents, seq_len = inputs_one
        weight = (positions < seq_len).astype(jnp.float32) / seq_len.astype(jnp.float32)
        reduced_hidden = jnp.dot(sequence_activations, adapter_down, preferred_element_type=jnp.float32)
        reduced_upstream = jnp.dot(sequence_cotangents, adapter_up.T, preferred_element_type=jnp.float32)
        hidden_w = (reduced_hidden * weight[:, None]).astype(jnp.bfloat16)
        upper_w = (reduced_upstream * weight[:, None]).astype(jnp.bfloat16)
        grad_a = jnp.dot(sequence_activations.T, upper_w, preferred_element_type=jnp.float32)
        grad_b = jnp.dot(sequence_cotangents.T, hidden_w, preferred_element_type=jnp.float32)
        return jnp.concatenate([grad_a, grad_b], axis=1).astype(jnp.bfloat16)

    gradient_list = lax.map(one_sequence, (acts, cotangent, lengths))
    strata = WPARTS * RPARTS
    by_range = gradient_list.reshape(SEQS, strata, ROWS, 2 * ADAPTER_RANK).transpose(1, 0, 2, 3)
    row_pick = projection_rows.reshape(strata, NB_OUT)
    block_list = projection_blocks.reshape(strata, NB_OUT, 2 * ADAPTER_RANK, OB)

    def add_range(running, item_one):
        section, picks, block_one = item_one
        chosen = jnp.take(section, picks, axis=1)
        contrib = jnp.einsum("eok,okc->eoc", chosen.astype(jnp.float32), block_one.astype(jnp.float32),
                             precision=lax.Precision.HIGHEST)
        return running + contrib.reshape(SEQS, NB_OUT * OB), None

    start_sum = jnp.zeros((SEQS, NB_OUT * OB), jnp.float32)
    features, _ = lax.scan(add_range, start_sum, (by_range, row_pick, block_list))
    return features
```

```python
import functools

import jax
import jax.numpy as jnp
from jax import lax
from jax.experimental import pallas as pl
from jax.experimental.pallas import tpu as pltpu
from jax.sharding import PartitionSpec as P

MESH = pl.DeviceIdType.MESH
F32 = jnp.float32
BF16 = jnp.bfloat16
SEQ = 5
GROUPS = 32
CHIPS = 16


def group_of(y, x, core):
    return ((y // 2 * 4 + x) * 2 + core) * 2 + y % 2


def kernel(
    acts, cot, down, up, lens, rows, blocks, out,
    a_buf, c_buf, b_buf, own, relay_f, part, relay_in, fin_in, gath, grads, land, turned,
    contrib, cross, summed, plane, fsend, frecv,
    load_sem, block_sem, rs_send, rs_recv, ag_send, ag_recv, a2a_send, a2a_recv,
    cross_sem, plane_send, plane_recv, fin_send, fin_recv,
):
    dp, pj, me = lax.axis_index("dp"), lax.axis_index("proj"), lax.axis_index("tensor")
    group = dp * 2 + pj
    core = dp % 2
    xx = (dp // 2) % 4
    yy = (dp // 8) * 2 + pj
    chip = (dp // 2) * 2 + pj
    right, left, far = (me + 1) % 4, (me + 3) % 4, (me + 2) % 4

    def at(g, z):
        return {"dp": g // 2, "proj": g % 2, "tensor": z}

    def peer(k):
        return group_of((yy + k // 8) % 4, (xx + (k // 2) % 4) % 4, (core + k % 2) % 2)

    def back(k):
        return group_of((yy + 4 - k // 8) % 4, (xx + 4 - (k // 2) % 4) % 4, (core + k % 2) % 2)

    def loads(e):
        return (
            pltpu.make_async_copy(acts.at[e], a_buf.at[e], load_sem.at[0, e]),
            pltpu.make_async_copy(cot.at[e], c_buf.at[e], load_sem.at[1, e]),
        )

    for e in range(SEQ):
        for copy in loads(e):
            copy.start()
    block_load = pltpu.make_async_copy(blocks, b_buf, block_sem)
    block_load.start()

    barrier = pltpu.get_barrier_semaphore()

    def greet(k, _):
        pl.semaphore_signal(barrier, inc=1, device_id=at(back(k), me), device_id_type=MESH)
        return 0

    lax.fori_loop(1, GROUPS, greet, 0)
    for z in (left, right):
        pl.semaphore_signal(barrier, inc=1, device_id=at(group, z), device_id_type=MESH)

    def greet_final(k, _):
        g, z = me * 8 + k // 4, k % 4

        @pl.when(jnp.logical_or(g != group, z != me))
        def _():
            pl.semaphore_signal(barrier, inc=1, device_id=at(g, z), device_id_type=MESH)

        return 0

    lax.fori_loop(0, 32, greet_final, 0)
    goal = group // 8
    pl.semaphore_wait(barrier, 31 + 2 + jnp.where(goal == me, 31, 32))

    def remote(src, dst, send, recv, g, z):
        return pltpu.make_async_remote_copy(
            src_ref=src, dst_ref=dst, send_sem=send, recv_sem=recv, device_id=at(g, z), device_id_type=MESH
        )

    def rs_copy(e, n):
        src, dst, z = (
            lambda: (part.at[e, far, 0], relay_in.at[e, 1], left),
            lambda: (part.at[e, far, 1], relay_in.at[e, 0], right),
            lambda: (part.at[e, right, 0], fin_in.at[e, 0], right),
            lambda: (part.at[e, left, 1], fin_in.at[e, 3], left),
            lambda: (part.at[e, right, 1], fin_in.at[e, 1], right),
            lambda: (part.at[e, left, 0], fin_in.at[e, 2], left),
        )[n]()
        return remote(src, dst, rs_send.at[e, n], rs_recv.at[e, n], group, z)

    def ag_copy(e, n):
        q, half, z = (
            (me, 0, right), (me, 1, left), (me, 1, right), (me, 0, left), (left, 0, right), (right, 1, left),
        )[n]
        block = gath.at[e, q * 2 + half]
        return remote(block, block, ag_send.at[e, n], ag_recv.at[e, n], group, z)

    def a2a_copy(e, k):
        g = peer(k)
        return remote(grads.at[e, g], land.at[e, group], a2a_send.at[e], a2a_recv.at[e], g, me)

    def low(e):
        for copy in loads(e):
            copy.wait()

        def partial(q):
            h = jnp.dot(a_buf[e, q], down[...], preferred_element_type=F32)
            u = lax.dot_general(c_buf[e, q], up[...], (((1,), (1,)), ((), ())), preferred_element_type=F32)
            return h, u

        h, u = partial(far)
        part[e, far, :, :, 0:128] = h.astype(BF16).reshape(2, 128, 128)
        part[e, far, :, :, 128:256] = u.astype(BF16).reshape(2, 128, 128)
        rs_copy(e, 0).start()
        rs_copy(e, 1).start()
        h, u = partial(right)
        part[e, right, 0, :, 0:128] = h[0:128].astype(BF16)
        part[e, right, 0, :, 128:256] = u[0:128].astype(BF16)
        relay_f[e, 0, :, 0:128] = h[128:256]
        relay_f[e, 0, :, 128:256] = u[128:256]
        rs_copy(e, 2).start()
        h, u = partial(left)
        part[e, left, 1, :, 0:128] = h[128:256].astype(BF16)
        part[e, left, 1, :, 128:256] = u[128:256].astype(BF16)
        relay_f[e, 1, :, 0:128] = h[0:128]
        relay_f[e, 1, :, 128:256] = u[0:128]
        rs_copy(e, 3).start()
        h, u = partial(me)
        own[e, :, 0:128] = h
        own[e, :, 128:256] = u

    def relay(e):
        rs_copy(e, 1).wait_recv()
        part[e, right, 1] = (relay_f[e, 0] + relay_in[e, 0].astype(F32)).astype(BF16)
        rs_copy(e, 4).start()
        rs_copy(e, 0).wait_recv()
        part[e, left, 0] = (relay_f[e, 1] + relay_in[e, 1].astype(F32)).astype(BF16)
        rs_copy(e, 5).start()

    def finish(e):
        length = jnp.full((128, 256), lens[e], jnp.int32)

        def half(n, first, second):
            place = lax.broadcasted_iota(jnp.int32, (128, 256), 0) + (me * 256 + n * 128)
            weight = jnp.where(place < length, 1.0 / length.astype(F32), 0.0)
            total = own[e, n * 128 : n * 128 + 128] + (fin_in[e, first].astype(F32) + fin_in[e, second].astype(F32))
            gath[e, me * 2 + n] = (total * weight).astype(BF16)

        rs_copy(e, 2).wait_recv()
        rs_copy(e, 5).wait_recv()
        half(0, 0, 2)
        ag_copy(e, 0).start()
        rs_copy(e, 3).wait_recv()
        rs_copy(e, 4).wait_recv()
        half(1, 3, 1)
        ag_copy(e, 1).start()
        ag_copy(e, 2).start()
        ag_copy(e, 3).start()

    def forward(e):
        ag_copy(e, 0).wait_recv()
        ag_copy(e, 4).start()
        ag_copy(e, 1).wait_recv()
        ag_copy(e, 5).start()

    def gradient(e):
        for n in (2, 3, 4, 5):
            ag_copy(e, n).wait_recv()
        for side in (0, 1):
            buf = (a_buf, c_buf)[side]
            other = gath[e, :, :, 128 - side * 128 : 256 - side * 128].reshape(1024, 128)

            def tile(w, _):
                wide = buf[e, :, :, pl.ds(pl.multiple_of(w * 256, 256), 256)].reshape(1024, 256)
                g = lax.dot_general(wide, other, (((0,), (0,)), ((), ())), preferred_element_type=F32)
                grads[e, pl.ds(w * 8, 8), :, side * 128 : side * 128 + 128] = g.astype(BF16).reshape(8, 32, 128)
                return 0

            lax.fori_loop(0, 4, tile, 0)

        pltpu.make_async_copy(grads.at[e, group], land.at[e, group], a2a_recv.at[e]).start()

        def send(k, _):
            a2a_copy(e, k).start()
            return 0

        lax.fori_loop(1, GROUPS, send, 0)

    def turn(e):
        pltpu.make_async_copy(land.at[e], land.at[e], a2a_recv.at[e]).wait()
        turned[:, e] = jnp.swapaxes(land[e].astype(F32), 0, 1).astype(BF16)

    stages = (low, relay, finish, forward, gradient, turn)

    def step(s, _):
        for lag, stage in enumerate(stages):

            @pl.when(jnp.logical_and(s >= lag, s < lag + SEQ))
            def _(lag=lag, stage=stage):
                stage(s - lag)

        return 0

    lax.fori_loop(0, SEQ + len(stages) - 1, step, 0)

    block_load.wait()

    def project(n, _):
        o_core, o_chip, i = n // 32, (n // 2) % 16, n % 2
        o = ((o_chip // 2) * 4 + o_core * 2 + o_chip % 2) * 2 + i
        picked = turned[rows[o]].reshape(SEQ * GROUPS, 256)
        contrib[o_core, o_chip, i] = jnp.dot(picked, b_buf[o], preferred_element_type=F32)
        return 0

    lax.fori_loop(0, 64, project, 0)

    sibling = group + 2 - 4 * core
    swap = remote(contrib.at[1 - core], cross, cross_sem.at[0], cross_sem.at[1], sibling, me)
    swap.start()
    swap.wait()

    def add(p, _):
        summed[p] = (contrib[core, p] + cross[p]).astype(BF16)
        return 0

    lax.fori_loop(0, CHIPS, add, 0)

    def plane_copy(k):
        y, x = (yy + k // 4) % 4, (xx + k % 4) % 4
        to = (y // 2 * 4 + x) * 2 + y % 2
        return remote(
            summed.at[to], plane.at[k], plane_send.at[k], plane_recv.at[k], group_of(y, x, core), me
        )

    def plane_start(k, _):
        plane_copy(k).start()
        return 0

    lax.fori_loop(1, CHIPS, plane_start, 0)
    contrib[core, chip] = contrib[core, chip] + cross[chip]

    def plane_add(k, _):
        plane_copy(k).wait_recv()
        contrib[core, chip] = contrib[core, chip] + plane[k].astype(F32)
        return 0

    lax.fori_loop(1, CHIPS, plane_add, 0)

    for i in range(2):
        for e in range(SEQ):
            fsend[:, i, e, :] = contrib[core, chip, i, e * 32 : e * 32 + 32, :]

    def is_self(s):
        return jnp.logical_and(s == group, goal == me)

    def final_copy(s):
        slot = (group % 8) * 4 + me
        return remote(fsend.at[s], frecv.at[slot], fin_send, fin_recv, s, goal)

    def final_start(s, _):
        @pl.when(is_self(s))
        def _():
            slot = (group % 8) * 4 + me
            pltpu.make_async_copy(fsend.at[s], frecv.at[slot], fin_recv).start()

        @pl.when(jnp.logical_not(is_self(s)))
        def _():
            final_copy(s).start()

        return 0

    lax.fori_loop(0, GROUPS, final_start, 0)
    pltpu.make_async_copy(frecv, frecv, fin_recv).wait()
    for n in range(8):
        out[2 * n : 2 * n + 2] = (frecv[4 * n] + frecv[4 * n + 1]) + (frecv[4 * n + 2] + frecv[4 * n + 3])

    def drain(e, _):
        for n in range(6):
            rs_copy(e, n).wait_send()
            ag_copy(e, n).wait_send()
        pltpu.make_async_copy(
            land.at[e, pl.ds(0, 31)], land.at[e, pl.ds(0, 31)], a2a_send.at[e]
        ).wait()
        return 0

    lax.fori_loop(0, SEQ, drain, 0)

    def plane_drain(k, _):
        plane_copy(k).wait_send()
        return 0

    lax.fori_loop(1, CHIPS, plane_drain, 0)

    def final_drain(s, _):
        @pl.when(jnp.logical_not(is_self(s)))
        def _():
            final_copy(s).wait_send()

        return 0

    lax.fori_loop(0, GROUPS, final_drain, 0)


def local(acts, cotangent, adapter_down, adapter_up, lengths, projection_rows, projection_blocks):
    vmem, smem, hbm = (pl.BlockSpec(memory_space=m) for m in (pltpu.VMEM, pltpu.SMEM, pl.ANY))
    dma = pltpu.SemaphoreType.DMA
    out = pl.pallas_call(
        kernel,
        out_shape=jax.ShapeDtypeStruct((16, 8, 128), F32),
        in_specs=[hbm, hbm, vmem, vmem, smem, smem, hbm],
        out_specs=vmem,
        scratch_shapes=[
            pltpu.VMEM((SEQ, 4, 256, 1024), BF16),
            pltpu.VMEM((SEQ, 4, 256, 1024), BF16),
            pltpu.VMEM((64, 256, 128), BF16),
            pltpu.VMEM((SEQ, 256, 256), F32),
            pltpu.VMEM((SEQ, 2, 128, 256), F32),
            pltpu.VMEM((SEQ, 4, 2, 128, 256), BF16),
            pltpu.VMEM((SEQ, 2, 128, 256), BF16),
            pltpu.VMEM((SEQ, 4, 128, 256), BF16),
            pltpu.VMEM((SEQ, 8, 128, 256), BF16),
            pltpu.VMEM((SEQ, 32, 32, 256), BF16),
            pltpu.VMEM((SEQ, 32, 32, 256), BF16),
            pltpu.VMEM((32, SEQ, 32, 256), BF16),
            pltpu.VMEM((2, CHIPS, 2, SEQ * GROUPS, 128), F32),
            pltpu.VMEM((CHIPS, 2, SEQ * GROUPS, 128), F32),
            pltpu.VMEM((CHIPS, 2, SEQ * GROUPS, 128), BF16),
            pltpu.VMEM((CHIPS, 2, SEQ * GROUPS, 128), BF16),
            pltpu.VMEM((GROUPS, 2, 8, 128), F32),
            pltpu.VMEM((32, 2, 8, 128), F32),
            dma((2, SEQ)), dma, dma((SEQ, 6)), dma((SEQ, 6)), dma((SEQ, 6)), dma((SEQ, 6)), dma((SEQ,)), dma((SEQ,)),
            dma((2,)), dma((CHIPS,)), dma((CHIPS,)), dma, dma,
        ],
        compiler_params=pltpu.CompilerParams(
            collective_id=0, has_side_effects=True, vmem_limit_bytes=60 * 1024 * 1024
        ),
        cost_estimate=pl.CostEstimate(flops=6 * 10**9, bytes_accessed=25 * 10**6, transcendentals=0),
    )(
        acts.reshape(SEQ, 4, 256, 1024),
        cotangent.reshape(SEQ, 4, 256, 1024),
        adapter_down,
        adapter_up,
        lengths,
        projection_rows.reshape(64),
        projection_blocks.reshape(64, 256, 128),
    )
    return jnp.swapaxes(out, 0, 1)[:SEQ].reshape(SEQ, 2048)


def solution(mesh):
    placed = (
        P(("dp", "proj"), None, "tensor"),
        P(("dp", "proj"), None, "tensor"),
        P("tensor", None),
        P(None, "tensor"),
        P(("dp", "proj")),
        P("tensor", ("dp", "proj"), None),
        P("tensor", ("dp", "proj"), None, None, None),
    )
    return jax.shard_map(
        local, mesh=mesh, in_specs=placed, out_specs=P(("dp", "proj"), "tensor"), check_vma=False
    )
```

```python
import functools

import jax
import jax.numpy as jnp
from jax import lax
from jax.experimental import pallas as pl
from jax.experimental.pallas import tpu as pltpu
from jax.sharding import PartitionSpec as P

MESH = pl.DeviceIdType.MESH
F32 = jnp.float32
BF16 = jnp.bfloat16
SEQ = 5
CHIPS = 16


SHIFTS = (
    (1, 0), (0, 1), (3, 0), (0, 3), (1, 1), (3, 3), (1, 3), (3, 1),
    (2, 0), (0, 2), (2, 1), (1, 2), (2, 3), (3, 2), (2, 2),
)
PEERS = ((0, 0, 1),) + tuple((x, y, c) for x, y in SHIFTS for c in (0, 1))


def kernel(
    acts, cot, down, up, lens, rows, blocks, out,
    a_buf, c_buf, b_buf, own, relay_f, part, relay_in, fin_in, gath, grads, land, turned,
    contrib, cross, swapped, summed, mine, plane, fsend, frecv,
    load_sem, block_sem, rs_send, rs_recv, ag_send, ag_recv, a2a_send, a2a_recv,
    cross_send, cross_recv, plane_send, plane_recv, fin_send, fin_recv,
):
    dp, pj, me = lax.axis_index("dp"), lax.axis_index("proj"), lax.axis_index("tensor")
    group = dp * 2 + pj
    core = lax.rem(dp, 2)
    xx = lax.rem(lax.div(dp, 2), 4)
    yy = lax.div(dp, 8) * 2 + pj
    xs = [lax.rem(xx + d, 4) for d in range(4)]
    ys = [lax.rem(yy + d, 4) for d in range(4)]
    yh = [lax.div(y, 2) for y in ys]
    yl = [lax.rem(y, 2) for y in ys]
    cores = (core, 1 - core)
    z_at = [lax.rem(me + d, 4) for d in range(4)]
    right, far, left = z_at[1:]

    def device(x, y, c, z=0):
        return {"dp": yh[y] * 8 + xs[x] * 2 + cores[c], "proj": yl[y], "tensor": z_at[z]}

    def rank(x, y, c):
        return (yh[y] * 8 + xs[x] * 2 + cores[c]) * 2 + yl[y]

    def chip_at(x, y):
        return (yh[y] * 4 + xs[x]) * 2 + yl[y]

    place = chip_at(0, 0) * 2 + core

    def loads(e):
        return (
            pltpu.make_async_copy(acts.at[e], a_buf.at[e], load_sem.at[0, e]),
            pltpu.make_async_copy(cot.at[e], c_buf.at[e], load_sem.at[1, e]),
        )

    for e in range(SEQ):
        for copy in loads(e):
            copy.start()
    block_load = pltpu.make_async_copy(blocks, b_buf, block_sem)
    block_load.start()

    barrier = pltpu.get_barrier_semaphore()
    others = [device(x, y, c) for x, y, c in PEERS] + [device(0, 0, c, z) for c in (0, 1) for z in (1, 2, 3)]
    for other in others:
        pl.semaphore_signal(barrier, inc=1, device_id=other, device_id_type=MESH)
    pl.semaphore_wait(barrier, len(others))

    def remote(src, dst, send, recv, to):
        return pltpu.make_async_remote_copy(
            src_ref=src, dst_ref=dst, send_sem=send, recv_sem=recv, device_id=to, device_id_type=MESH
        )

    def rs_copy(e, n):
        src, dst, z = (
            lambda: (part.at[e, far, 0], relay_in.at[e, 1], 3),
            lambda: (part.at[e, far, 1], relay_in.at[e, 0], 1),
            lambda: (part.at[e, right, 0], fin_in.at[e, 0], 1),
            lambda: (part.at[e, left, 1], fin_in.at[e, 3], 3),
            lambda: (part.at[e, right, 1], fin_in.at[e, 1], 1),
            lambda: (part.at[e, left, 0], fin_in.at[e, 2], 3),
        )[n]()
        return remote(src, dst, rs_send.at[e, n], rs_recv.at[e, n], device(0, 0, 0, z))

    def ag_copy(e, n):
        q, half, z = ((me, 0, 1), (me, 1, 3), (me, 1, 1), (me, 0, 3), (left, 0, 1), (right, 1, 3))[n]
        block = gath.at[e, q * 2 + half]
        return remote(block, block, ag_send.at[e, n], ag_recv.at[e, n], device(0, 0, 0, z))

    def low(e):
        for copy in loads(e):
            copy.wait()

        def partial(q):
            h = jnp.dot(a_buf[e, q], down[...], preferred_element_type=F32)
            u = lax.dot_general(c_buf[e, q], up[...], (((1,), (1,)), ((), ())), preferred_element_type=F32)
            return h, u

        h, u = partial(far)
        part[e, far, :, :, 0:128] = h.astype(BF16).reshape(2, 128, 128)
        part[e, far, :, :, 128:256] = u.astype(BF16).reshape(2, 128, 128)
        rs_copy(e, 0).start()
        rs_copy(e, 1).start()
        h, u = partial(right)
        part[e, right, 0, :, 0:128] = h[0:128].astype(BF16)
        part[e, right, 0, :, 128:256] = u[0:128].astype(BF16)
        relay_f[e, 0, :, 0:128] = h[128:256]
        relay_f[e, 0, :, 128:256] = u[128:256]
        rs_copy(e, 2).start()
        h, u = partial(left)
        part[e, left, 1, :, 0:128] = h[128:256].astype(BF16)
        part[e, left, 1, :, 128:256] = u[128:256].astype(BF16)
        relay_f[e, 1, :, 0:128] = h[0:128]
        relay_f[e, 1, :, 128:256] = u[0:128]
        rs_copy(e, 3).start()
        h, u = partial(me)
        own[e, :, 0:128] = h
        own[e, :, 128:256] = u

    def relay(e):
        rs_copy(e, 1).wait_recv()
        part[e, right, 1] = (relay_f[e, 0] + relay_in[e, 0].astype(F32)).astype(BF16)
        rs_copy(e, 4).start()
        rs_copy(e, 0).wait_recv()
        part[e, left, 0] = (relay_f[e, 1] + relay_in[e, 1].astype(F32)).astype(BF16)
        rs_copy(e, 5).start()

    def finish(e):
        length = jnp.full((128, 256), lens[e], jnp.int32)

        def half(n, first, second):
            token = lax.broadcasted_iota(jnp.int32, (128, 256), 0) + (me * 256 + n * 128)
            weight = jnp.where(token < length, 1.0 / length.astype(F32), 0.0)
            total = own[e, n * 128 : n * 128 + 128] + (fin_in[e, first].astype(F32) + fin_in[e, second].astype(F32))
            gath[e, me * 2 + n] = (total * weight).astype(BF16)

        rs_copy(e, 2).wait_recv()
        rs_copy(e, 5).wait_recv()
        half(0, 0, 2)
        ag_copy(e, 0).start()
        rs_copy(e, 3).wait_recv()
        rs_copy(e, 4).wait_recv()
        half(1, 3, 1)
        ag_copy(e, 1).start()
        ag_copy(e, 2).start()
        ag_copy(e, 3).start()

    def forward(e):
        ag_copy(e, 0).wait_recv()
        ag_copy(e, 4).start()
        ag_copy(e, 1).wait_recv()
        ag_copy(e, 5).start()

    def gradient(e):
        for n in (2, 3, 4, 5):
            ag_copy(e, n).wait_recv()
        for side in (0, 1):
            buf = (a_buf, c_buf)[side]
            other = gath[e, :, :, 128 - side * 128 : 256 - side * 128].reshape(1024, 128).T
            for w in range(4):
                wide = buf[e, :, :, w * 256 : w * 256 + 256].reshape(1024, 256)
                g = jnp.dot(other, wide, preferred_element_type=F32).T
                grads[e, w * 8 : w * 8 + 8, :, side * 128 : side * 128 + 128] = g.astype(BF16).reshape(8, 32, 128)
        pltpu.make_async_copy(grads.at[e, group], land.at[e, place], a2a_recv.at[e]).start()
        for x, y, c in PEERS:
            remote(
                grads.at[e, rank(x, y, c)], land.at[e, place], a2a_send.at[e], a2a_recv.at[e], device(x, y, c)
            ).start()

    def swap(e):
        return remote(
            contrib.at[e, 1 - core], cross.at[e], cross_send.at[e], cross_recv.at[e], device(0, 0, 1)
        )

    def project(e):
        pltpu.make_async_copy(land.at[e], land.at[e], a2a_recv.at[e]).wait()
        turned[...] = jnp.swapaxes(land[e].astype(F32), 0, 1).astype(BF16)

        def half(h):
            def one(n, _):
                o = lax.div(n, 8) * 16 + h * 8 + lax.rem(n, 8)
                contrib[e, h, n] = jnp.dot(turned[rows[o]], b_buf[o], preferred_element_type=F32)
                return 0

            lax.fori_loop(0, 32, one, 0, unroll=16)

        half(1 - core)
        swap(e).start()
        half(core)

    def scatter(e):
        swap(e).wait_recv()
        swapped[...] = jnp.swapaxes(contrib[e, core] + cross[e], 0, 1)
        summed[e] = swapped[...].astype(BF16).reshape(CHIPS, 2, 32, 128)
        for k, (x, y) in enumerate(SHIFTS):
            remote(
                summed.at[e, chip_at(x, y)], plane.at[e, k], plane_send.at[e], plane_recv.at[e], device(x, y, 0)
            ).start()
        for k in range(2):
            mine[e, k] = swapped[chip_at(0, 0) * 2 + k]

    def collect(e):
        pltpu.make_async_copy(plane.at[e], plane.at[e], plane_recv.at[e]).wait()
        total = mine[e]
        for k in range(len(SHIFTS)):
            total = total + plane[e, k].astype(F32)
        fsend[e] = total.reshape(2, 4, 8, 128)
        for c in (0, 1):
            for z in range(4):
                src, dst = fsend.at[e, cores[c], z_at[z]], frecv.at[e, core, me]
                if c == 0 and z == 0:
                    pltpu.make_async_copy(src, dst, fin_recv.at[e]).start()
                else:
                    remote(src, dst, fin_send.at[e], fin_recv.at[e], device(0, 0, c, z)).start()

    stages = (low, relay, finish, forward, gradient, project, scatter, collect)

    def step(s, _):
        @pl.when(s == 5)
        def _():
            block_load.wait()

        for lag, stage in enumerate(stages):

            @pl.when(jnp.logical_and(s >= lag, s < lag + SEQ))
            def _(lag=lag, stage=stage):
                stage(s - lag)

        return 0

    lax.fori_loop(0, SEQ + len(stages) - 1, step, 0)

    for e in range(SEQ):
        pltpu.make_async_copy(frecv.at[e], frecv.at[e], fin_recv.at[e]).wait()
        for h in range(2):
            out[e, h * 8 : h * 8 + 8] = (frecv[e, h, 0] + frecv[e, h, 1]) + (frecv[e, h, 2] + frecv[e, h, 3])

    def drain(e, _):
        for n in range(6):
            rs_copy(e, n).wait_send()
            ag_copy(e, n).wait_send()
        swap(e).wait_send()
        for ref, sem in (
            (land.at[e, pl.ds(0, 31)], a2a_send.at[e]),
            (plane.at[e], plane_send.at[e]),
            (fsend.at[e, 0, pl.ds(0, 3)], fin_send.at[e]),
            (fsend.at[e, 1], fin_send.at[e]),
        ):
            pltpu.make_async_copy(ref, ref, sem).wait()
        return 0

    lax.fori_loop(0, SEQ, drain, 0)


def local(acts, cotangent, adapter_down, adapter_up, lengths, projection_rows, projection_blocks):
    vmem, smem, hbm = (pl.BlockSpec(memory_space=m) for m in (pltpu.VMEM, pltpu.SMEM, pl.ANY))
    dma = pltpu.SemaphoreType.DMA
    out = pl.pallas_call(
        kernel,
        out_shape=jax.ShapeDtypeStruct((SEQ, 16, 128), F32),
        in_specs=[hbm, hbm, vmem, vmem, smem, smem, hbm],
        out_specs=vmem,
        scratch_shapes=[
            pltpu.VMEM((SEQ, 4, 256, 1024), BF16),
            pltpu.VMEM((SEQ, 4, 256, 1024), BF16),
            pltpu.VMEM((64, 256, 128), BF16),
            pltpu.VMEM((SEQ, 256, 256), F32),
            pltpu.VMEM((SEQ, 2, 128, 256), F32),
            pltpu.VMEM((SEQ, 4, 2, 128, 256), BF16),
            pltpu.VMEM((SEQ, 2, 128, 256), BF16),
            pltpu.VMEM((SEQ, 4, 128, 256), BF16),
            pltpu.VMEM((SEQ, 8, 128, 256), BF16),
            pltpu.VMEM((SEQ, 32, 32, 256), BF16),
            pltpu.VMEM((SEQ, 32, 32, 256), BF16),
            pltpu.VMEM((32, 32, 256), BF16),
            pltpu.VMEM((SEQ, 2, 32, 32, 128), F32),
            pltpu.VMEM((SEQ, 32, 32, 128), F32),
            pltpu.VMEM((32, 32, 128), F32),
            pltpu.VMEM((SEQ, CHIPS, 2, 32, 128), BF16),
            pltpu.VMEM((SEQ, 2, 32, 128), F32),
            pltpu.VMEM((SEQ, CHIPS - 1, 2, 32, 128), BF16),
            pltpu.VMEM((SEQ, 2, 4, 8, 128), F32),
            pltpu.VMEM((SEQ, 2, 4, 8, 128), F32),
            dma((2, SEQ)), dma, dma((SEQ, 6)), dma((SEQ, 6)), dma((SEQ, 6)), dma((SEQ, 6)), dma((SEQ,)), dma((SEQ,)),
            dma((SEQ,)), dma((SEQ,)), dma((SEQ,)), dma((SEQ,)), dma((SEQ,)), dma((SEQ,)),
        ],
        compiler_params=pltpu.CompilerParams(
            collective_id=0, has_side_effects=True, vmem_limit_bytes=60 * 1024 * 1024
        ),
        cost_estimate=pl.CostEstimate(flops=6 * 10**9, bytes_accessed=25 * 10**6, transcendentals=0),
    )(
        acts.reshape(SEQ, 4, 256, 1024),
        cotangent.reshape(SEQ, 4, 256, 1024),
        adapter_down,
        adapter_up,
        lengths,
        projection_rows.reshape(64),
        projection_blocks.reshape(64, 256, 128),
    )
    return out.reshape(SEQ, 2048)


def solution(mesh):
    placed = (
        P(("dp", "proj"), None, "tensor"),
        P(("dp", "proj"), None, "tensor"),
        P("tensor", None),
        P(None, "tensor"),
        P(("dp", "proj")),
        P("tensor", ("dp", "proj"), None),
        P("tensor", ("dp", "proj"), None, None, None),
    )
    return jax.shard_map(
        local, mesh=mesh, in_specs=placed, out_specs=P(("dp", "proj"), "tensor"), check_vma=False
    )
```

```python
import functools

import jax
import jax.numpy as jnp
from jax import lax
from jax.experimental import pallas as pl
from jax.experimental.pallas import tpu as pltpu
from jax.sharding import PartitionSpec as P

MESH = pl.DeviceIdType.MESH
F32 = jnp.float32
BF16 = jnp.bfloat16
SEQ = 5
CHIPS = 16


SHIFTS = (
    (2, 2), (3, 2), (2, 3), (1, 2), (2, 1), (0, 2), (2, 0), (3, 1),
    (1, 3), (3, 3), (1, 1), (0, 3), (3, 0), (0, 1), (1, 0),
)
PEERS = tuple((x, y, c) for x, y in SHIFTS for c in (0, 1)) + ((0, 0, 1),)


def kernel(
    acts, cot, down, up, lens, rows, blocks, out,
    a_buf, c_buf, b_buf, own, relay_f, part, relay_in, fin_in, gath, grads, land, turned,
    contrib, cross, swapped, summed, mine, plane, fsend, frecv,
    load_sem, block_sem, rs_send, rs_recv, ag_send, ag_recv, a2a_send, a2a_recv,
    cross_send, cross_recv, plane_send, plane_recv, fin_send, fin_recv,
):
    dp, pj, me = lax.axis_index("dp"), lax.axis_index("proj"), lax.axis_index("tensor")
    group = dp * 2 + pj
    core = lax.rem(dp, 2)
    xx = lax.rem(lax.div(dp, 2), 4)
    yy = lax.div(dp, 8) * 2 + pj
    xs = [lax.rem(xx + d, 4) for d in range(4)]
    ys = [lax.rem(yy + d, 4) for d in range(4)]
    yh = [lax.div(y, 2) for y in ys]
    yl = [lax.rem(y, 2) for y in ys]
    cores = (core, 1 - core)
    z_at = [lax.rem(me + d, 4) for d in range(4)]
    right, far, left = z_at[1:]

    def device(x, y, c, z=0):
        return {"dp": yh[y] * 8 + xs[x] * 2 + cores[c], "proj": yl[y], "tensor": z_at[z]}

    def rank(x, y, c):
        return (yh[y] * 8 + xs[x] * 2 + cores[c]) * 2 + yl[y]

    def chip_at(x, y):
        return (yh[y] * 4 + xs[x]) * 2 + yl[y]

    place = chip_at(0, 0) * 2 + core

    def loads(e):
        return (
            pltpu.make_async_copy(acts.at[e], a_buf.at[e], load_sem.at[0, e]),
            pltpu.make_async_copy(cot.at[e], c_buf.at[e], load_sem.at[1, e]),
        )

    for copy in loads(0):
        copy.start()
    block_load = pltpu.make_async_copy(blocks, b_buf, block_sem)

    barrier = pltpu.get_barrier_semaphore()
    others = [device(x, y, c) for x, y, c in PEERS] + [device(0, 0, c, z) for c in (0, 1) for z in (1, 2, 3)]
    for other in others:
        pl.semaphore_signal(barrier, inc=1, device_id=other, device_id_type=MESH)
    for e in range(1, SEQ):
        for copy in loads(e):
            copy.start()
    block_load.start()

    def remote(src, dst, send, recv, to):
        return pltpu.make_async_remote_copy(
            src_ref=src, dst_ref=dst, send_sem=send, recv_sem=recv, device_id=to, device_id_type=MESH
        )

    def rs_copy(e, n):
        src, dst, z = (
            lambda: (part.at[e, far, 0], relay_in.at[e, 1], 3),
            lambda: (part.at[e, far, 1], relay_in.at[e, 0], 1),
            lambda: (part.at[e, right, 0], fin_in.at[e, 0], 1),
            lambda: (part.at[e, left, 1], fin_in.at[e, 3], 3),
            lambda: (part.at[e, right, 1], fin_in.at[e, 1], 1),
            lambda: (part.at[e, left, 0], fin_in.at[e, 2], 3),
        )[n]()
        return remote(src, dst, rs_send.at[e, n], rs_recv.at[e, n], device(0, 0, 0, z))

    def ag_copy(e, z):
        return remote(
            gath.at[e, me], gath.at[e, me], ag_send.at[e, z - 1], ag_recv.at[e, z - 1], device(0, 0, 0, z)
        )

    def partial(e, q):
        h = jnp.dot(a_buf[e, q], down[...], preferred_element_type=F32)
        u = lax.dot_general(c_buf[e, q], up[...], (((1,), (1,)), ((), ())), preferred_element_type=F32)
        return h, u

    def far_sums(e):
        for copy in loads(e):
            copy.wait()
        h, u = partial(e, far)
        part[e, far, :, :, 0:128] = h.astype(BF16).reshape(2, 128, 128)
        part[e, far, :, :, 128:256] = u.astype(BF16).reshape(2, 128, 128)

    def near_sums(e):
        h, u = partial(e, right)
        part[e, right, 0, :, 0:128] = h[0:128].astype(BF16)
        part[e, right, 0, :, 128:256] = u[0:128].astype(BF16)
        relay_f[e, 0, :, 0:128] = h[128:256]
        relay_f[e, 0, :, 128:256] = u[128:256]
        h, u = partial(e, left)
        part[e, left, 1, :, 0:128] = h[128:256].astype(BF16)
        part[e, left, 1, :, 128:256] = u[128:256].astype(BF16)
        relay_f[e, 1, :, 0:128] = h[0:128]
        relay_f[e, 1, :, 128:256] = u[0:128]

    def low_far(e):
        if e:
            far_sums(e)
        rs_copy(e, 0).start()
        rs_copy(e, 1).start()

    def low_near(e):
        if e:
            near_sums(e)
        rs_copy(e, 2).start()
        rs_copy(e, 3).start()
        h, u = partial(e, me)
        own[e, :, 0:128] = h
        own[e, :, 128:256] = u

    def relay(e):
        rs_copy(e, 1).wait_recv()
        part[e, right, 1] = (relay_f[e, 0] + relay_in[e, 0].astype(F32)).astype(BF16)
        rs_copy(e, 4).start()
        rs_copy(e, 0).wait_recv()
        part[e, left, 0] = (relay_f[e, 1] + relay_in[e, 1].astype(F32)).astype(BF16)
        rs_copy(e, 5).start()

    def finish(e):
        length = jnp.full((128, 256), lens[e], jnp.int32)

        def half(n, first, second):
            token = lax.broadcasted_iota(jnp.int32, (128, 256), 0) + (me * 256 + n * 128)
            weight = jnp.where(token < length, 1.0 / length.astype(F32), 0.0)
            total = own[e, n * 128 : n * 128 + 128] + (fin_in[e, first].astype(F32) + fin_in[e, second].astype(F32))
            gath[e, me, n * 128 : n * 128 + 128] = (total * weight).astype(BF16)

        for n in (2, 5, 3, 4):
            rs_copy(e, n).wait_recv()
        half(0, 0, 2)
        half(1, 3, 1)
        for z in (2, 1, 3):
            ag_copy(e, z).start()

    def gradient(e):
        for z in (1, 3, 2):
            ag_copy(e, z).wait_recv()
        for side in (0, 1):
            buf = (a_buf, c_buf)[side]
            other = gath[e, :, :, 128 - side * 128 : 256 - side * 128].reshape(1024, 128).T
            for w in range(4):
                wide = buf[e, :, :, w * 256 : w * 256 + 256].reshape(1024, 256)
                g = jnp.dot(other, wide, preferred_element_type=F32).T
                grads[e, w * 8 : w * 8 + 8, :, side * 128 : side * 128 + 128] = g.astype(BF16).reshape(8, 32, 128)
        pltpu.make_async_copy(grads.at[e, group], land.at[e, place], a2a_recv.at[e]).start()
        for x, y, c in PEERS:
            remote(
                grads.at[e, rank(x, y, c)], land.at[e, place], a2a_send.at[e], a2a_recv.at[e], device(x, y, c)
            ).start()

    def swap(e):
        return remote(
            contrib.at[e, 1 - core], cross.at[e], cross_send.at[e], cross_recv.at[e], device(0, 0, 1)
        )

    def blocks_ready(_):
        block_load.wait()

    def project(e):
        pltpu.make_async_copy(land.at[e], land.at[e], a2a_recv.at[e]).wait()
        turned[...] = jnp.swapaxes(land[e].astype(F32), 0, 1).astype(BF16)

        def half(h):
            def one(n, _):
                o = lax.div(n, 8) * 16 + h * 8 + lax.rem(n, 8)
                contrib[e, h, n] = jnp.dot(turned[rows[o]], b_buf[o], preferred_element_type=F32)
                return 0

            lax.fori_loop(0, 32, one, 0, unroll=16)

        half(1 - core)
        swap(e).start()
        half(core)

    def scatter(e):
        swap(e).wait_recv()
        swapped[...] = jnp.swapaxes(contrib[e, core] + cross[e], 0, 1)
        summed[e] = swapped[...].astype(BF16).reshape(CHIPS, 2, 32, 128)
        for k, (x, y) in enumerate(SHIFTS):
            remote(
                summed.at[e, chip_at(x, y)], plane.at[e, k], plane_send.at[e], plane_recv.at[e], device(x, y, 0)
            ).start()
        for k in range(2):
            mine[e, k] = swapped[chip_at(0, 0) * 2 + k]

    def collect(e):
        pltpu.make_async_copy(plane.at[e], plane.at[e], plane_recv.at[e]).wait()
        total = mine[e]
        for k in range(len(SHIFTS)):
            total = total + plane[e, k].astype(F32)
        fsend[e] = total.reshape(2, 4, 8, 128)
        for c in (0, 1):
            for z in range(4):
                src, dst = fsend.at[e, cores[c], z_at[z]], frecv.at[e, core, me]
                if c == 0 and z == 0:
                    pltpu.make_async_copy(src, dst, fin_recv.at[e]).start()
                else:
                    remote(src, dst, fin_send.at[e], fin_recv.at[e], device(0, 0, c, z)).start()

    far_sums(0)
    near_sums(0)
    pl.semaphore_wait(barrier, len(others))

    order = (
        (low_far, 0), (low_near, 0), (low_far, 1), (relay, 0), (low_near, 1), (relay, 1), (finish, 0),
        (low_far, 2), (finish, 1), (low_near, 2), (gradient, 0), (relay, 2), (low_far, 3), (low_near, 3),
        (gradient, 1), (finish, 2), (low_far, 4), (relay, 3), (blocks_ready, 0), (project, 0), (low_near, 4),
        (scatter, 0), (relay, 4), (gradient, 2), (finish, 3), (project, 1), (scatter, 1), (finish, 4),
        (collect, 0), (gradient, 3), (gradient, 4), (project, 2), (collect, 1), (scatter, 2), (project, 3),
        (scatter, 3), (project, 4), (scatter, 4), (collect, 2), (collect, 3), (collect, 4),
    )
    for stage, e in order:
        stage(e)

    for e in range(SEQ):
        pltpu.make_async_copy(frecv.at[e], frecv.at[e], fin_recv.at[e]).wait()
        for h in range(2):
            out[e, h * 8 : h * 8 + 8] = (frecv[e, h, 0] + frecv[e, h, 1]) + (frecv[e, h, 2] + frecv[e, h, 3])

    def drain(e, _):
        for n in range(6):
            rs_copy(e, n).wait_send()
        for z in (1, 2, 3):
            ag_copy(e, z).wait_send()
        swap(e).wait_send()
        for ref, sem in (
            (land.at[e, pl.ds(0, 31)], a2a_send.at[e]),
            (plane.at[e], plane_send.at[e]),
            (fsend.at[e, 0, pl.ds(0, 3)], fin_send.at[e]),
            (fsend.at[e, 1], fin_send.at[e]),
        ):
            pltpu.make_async_copy(ref, ref, sem).wait()
        return 0

    lax.fori_loop(0, SEQ, drain, 0)


def local(acts, cotangent, adapter_down, adapter_up, lengths, projection_rows, projection_blocks):
    vmem, smem, hbm = (pl.BlockSpec(memory_space=m) for m in (pltpu.VMEM, pltpu.SMEM, pl.ANY))
    dma = pltpu.SemaphoreType.DMA
    out = pl.pallas_call(
        kernel,
        out_shape=jax.ShapeDtypeStruct((SEQ, 16, 128), F32),
        in_specs=[hbm, hbm, vmem, vmem, smem, smem, hbm],
        out_specs=vmem,
        scratch_shapes=[
            pltpu.VMEM((SEQ, 4, 256, 1024), BF16),
            pltpu.VMEM((SEQ, 4, 256, 1024), BF16),
            pltpu.VMEM((64, 256, 128), BF16),
            pltpu.VMEM((SEQ, 256, 256), F32),
            pltpu.VMEM((SEQ, 2, 128, 256), F32),
            pltpu.VMEM((SEQ, 4, 2, 128, 256), BF16),
            pltpu.VMEM((SEQ, 2, 128, 256), BF16),
            pltpu.VMEM((SEQ, 4, 128, 256), BF16),
            pltpu.VMEM((SEQ, 4, 256, 256), BF16),
            pltpu.VMEM((SEQ, 32, 32, 256), BF16),
            pltpu.VMEM((SEQ, 32, 32, 256), BF16),
            pltpu.VMEM((32, 32, 256), BF16),
            pltpu.VMEM((SEQ, 2, 32, 32, 128), F32),
            pltpu.VMEM((SEQ, 32, 32, 128), F32),
            pltpu.VMEM((32, 32, 128), F32),
            pltpu.VMEM((SEQ, CHIPS, 2, 32, 128), BF16),
            pltpu.VMEM((SEQ, 2, 32, 128), F32),
            pltpu.VMEM((SEQ, CHIPS - 1, 2, 32, 128), BF16),
            pltpu.VMEM((SEQ, 2, 4, 8, 128), F32),
            pltpu.VMEM((SEQ, 2, 4, 8, 128), F32),
            dma((2, SEQ)), dma, dma((SEQ, 6)), dma((SEQ, 6)), dma((SEQ, 3)), dma((SEQ, 3)), dma((SEQ,)), dma((SEQ,)),
            dma((SEQ,)), dma((SEQ,)), dma((SEQ,)), dma((SEQ,)), dma((SEQ,)), dma((SEQ,)),
        ],
        compiler_params=pltpu.CompilerParams(
            collective_id=0, has_side_effects=True, vmem_limit_bytes=60 * 1024 * 1024
        ),
        cost_estimate=pl.CostEstimate(flops=6 * 10**9, bytes_accessed=25 * 10**6, transcendentals=0),
    )(
        acts.reshape(SEQ, 4, 256, 1024),
        cotangent.reshape(SEQ, 4, 256, 1024),
        adapter_down,
        adapter_up,
        lengths,
        projection_rows.reshape(64),
        projection_blocks.reshape(64, 256, 128),
    )
    return out.reshape(SEQ, 2048)


def solution(mesh):
    placed = (
        P(("dp", "proj"), None, "tensor"),
        P(("dp", "proj"), None, "tensor"),
        P("tensor", None),
        P(None, "tensor"),
        P(("dp", "proj")),
        P("tensor", ("dp", "proj"), None),
        P("tensor", ("dp", "proj"), None, None, None),
    )
    return jax.shard_map(
        local, mesh=mesh, in_specs=placed, out_specs=P(("dp", "proj"), "tensor"), check_vma=False
    )
```

```python
import functools

import jax
import jax.numpy as jnp
from jax import lax
from jax.experimental import pallas as pl
from jax.experimental.pallas import tpu as pltpu
from jax.sharding import PartitionSpec as P

MESH = pl.DeviceIdType.MESH
F32 = jnp.float32
BF16 = jnp.bfloat16
SEQ = 5
UNITS = ((0, 0, 256), (1, 0, 256), (2, 0, 256), (3, 0, 256), (4, 0, 128), (4, 128, 128))
COUNT = len(UNITS)
STRAIGHT = (COUNT - 1,)
CHIPS = 16


SHIFTS = (
    (2, 2), (3, 2), (2, 3), (1, 2), (2, 1), (0, 2), (2, 0), (3, 1),
    (1, 3), (3, 3), (1, 1), (0, 3), (3, 0), (0, 1), (1, 0),
)
PEERS = tuple((x, y, c) for x, y in SHIFTS for c in (0, 1)) + ((0, 0, 1),)


def kernel(
    acts, cot, down_in, up_in, lens_in, rows_in, blocks, out,
    a_buf, c_buf, b_buf, down, up, lens, rows, own, relay_f, part, relay_in, fin_in, gath, grads, land, turned,
    contrib, cross, swapped, summed, mine, plane, fsend, frecv,
    load_sem, small_sem, block_sem, rs_send, rs_recv, ag_send, ag_recv, a2a_send, a2a_recv,
    cross_send, cross_recv, plane_send, plane_recv, fin_send, fin_recv,
):
    dp, pj, me = lax.axis_index("dp"), lax.axis_index("proj"), lax.axis_index("tensor")
    group = dp * 2 + pj
    core = lax.rem(dp, 2)
    xx = lax.rem(lax.div(dp, 2), 4)
    yy = lax.div(dp, 8) * 2 + pj
    xs = [lax.rem(xx + d, 4) for d in range(4)]
    ys = [lax.rem(yy + d, 4) for d in range(4)]
    yh = [lax.div(y, 2) for y in ys]
    yl = [lax.rem(y, 2) for y in ys]
    cores = (core, 1 - core)
    z_at = [lax.rem(me + d, 4) for d in range(4)]
    right, far, left = z_at[1:]

    def device(x, y, c, z=0):
        return {"dp": yh[y] * 8 + xs[x] * 2 + cores[c], "proj": yl[y], "tensor": z_at[z]}

    def rank(x, y, c):
        return (yh[y] * 8 + xs[x] * 2 + cores[c]) * 2 + yl[y]

    def chip_at(x, y):
        return (yh[y] * 4 + xs[x]) * 2 + yl[y]

    place = chip_at(0, 0) * 2 + core

    def loads(e):
        return (
            pltpu.make_async_copy(acts.at[e], a_buf.at[e], load_sem.at[0, e]),
            pltpu.make_async_copy(cot.at[e], c_buf.at[e], load_sem.at[1, e]),
        )

    small = [
        pltpu.make_async_copy(src, dst, small_sem.at[n])
        for n, (src, dst) in enumerate(((down_in, down), (up_in, up), (lens_in, lens), (rows_in, rows)))
    ]
    small[0].start()
    loads(0)[0].start()
    small[1].start()
    loads(0)[1].start()
    small[2].start()
    small[3].start()
    block_load = pltpu.make_async_copy(blocks, b_buf, block_sem)

    barrier = pltpu.get_barrier_semaphore()
    others = [device(x, y, c) for x, y, c in PEERS] + [device(0, 0, c, z) for c in (0, 1) for z in (1, 2, 3)]
    for other in others:
        pl.semaphore_signal(barrier, inc=1, device_id=other, device_id_type=MESH)
    for e in range(1, SEQ):
        for copy in loads(e):
            copy.start()
    block_load.start()

    def remote(src, dst, send, recv, to):
        return pltpu.make_async_remote_copy(
            src_ref=src, dst_ref=dst, send_sem=send, recv_sem=recv, device_id=to, device_id_type=MESH
        )

    def rs_copy(i, n):
        e, column, width = UNITS[i]
        q, half, ref, slot, z = (
            (far, 0, relay_in, 1, 3),
            (far, 1, relay_in, 0, 1),
            (right, 0, fin_in, 0, 1),
            (left, 1, fin_in, 3, 3),
            (right, 1, fin_in, 1, 1),
            (left, 0, fin_in, 2, 3),
        )[n]
        columns = pl.ds(column, width)
        return remote(
            part.at[e, q, half, :, columns], ref.at[e, slot, :, columns], rs_send.at[i, n], rs_recv.at[i, n],
            device(0, 0, 0, z),
        )

    def straight_copy(i, z):
        e, column, width = UNITS[i]
        block = gath.at[e, me, :, pl.ds(column, width)]
        return remote(block, block, ag_send.at[i, z - 1], ag_recv.at[i, z - 1], device(0, 0, 0, z))

    def ag_copy(i, n):
        e, column, width = UNITS[i]
        q, half, z = ((me, 0, 1), (me, 1, 3), (me, 1, 1), (me, 0, 3), (left, 0, 1), (right, 1, 3))[n]
        block = gath.at[e, q, pl.ds(half * 128, 128), pl.ds(column, width)]
        return remote(block, block, ag_send.at[i, n], ag_recv.at[i, n], device(0, 0, 0, z))

    def partial(i, q):
        e, column, width = UNITS[i]
        if column == 0:
            yield 0, jnp.dot(a_buf[e, q], down[...], preferred_element_type=F32)
        if column + width == 256:
            yield 128, lax.dot_general(c_buf[e, q], up[...], (((1,), (1,)), ((), ())), preferred_element_type=F32)

    def far_sums(i):
        e, column, width = UNITS[i]
        for side in range(column // 128, (column + width) // 128):
            loads(e)[side].wait()
        for c, value in partial(i, far):
            part[e, far, :, :, c : c + 128] = value.astype(BF16).reshape(2, 128, 128)

    def near_sums(i):
        e = UNITS[i][0]
        for c, value in partial(i, right):
            part[e, right, 0, :, c : c + 128] = value[0:128].astype(BF16)
            relay_f[e, 0, :, c : c + 128] = value[128:256]
        for c, value in partial(i, left):
            part[e, left, 1, :, c : c + 128] = value[128:256].astype(BF16)
            relay_f[e, 1, :, c : c + 128] = value[0:128]

    def low_far(i):
        if i:
            far_sums(i)
        rs_copy(i, 0).start()
        rs_copy(i, 1).start()

    def low_near(i):
        if i:
            near_sums(i)
        rs_copy(i, 2).start()
        rs_copy(i, 3).start()
        for c, value in partial(i, me):
            own[UNITS[i][0], :, c : c + 128] = value

    def relay(i):
        e, column, width = UNITS[i]
        to = column + width
        rs_copy(i, 1).wait_recv()
        part[e, right, 1, :, column:to] = (
            relay_f[e, 0, :, column:to] + relay_in[e, 0, :, column:to].astype(F32)
        ).astype(BF16)
        rs_copy(i, 4).start()
        rs_copy(i, 0).wait_recv()
        part[e, left, 0, :, column:to] = (
            relay_f[e, 1, :, column:to] + relay_in[e, 1, :, column:to].astype(F32)
        ).astype(BF16)
        rs_copy(i, 5).start()

    def finish(i):
        e, column, width = UNITS[i]
        to = column + width
        length = jnp.full((128, width), lens[e], jnp.int32)

        def half(n, first, second):
            token = lax.broadcasted_iota(jnp.int32, (128, width), 0) + (me * 256 + n * 128)
            weight = jnp.where(token < length, 1.0 / length.astype(F32), 0.0)
            total = own[e, n * 128 : n * 128 + 128, column:to] + (
                fin_in[e, first, :, column:to].astype(F32) + fin_in[e, second, :, column:to].astype(F32)
            )
            gath[e, me, n * 128 : n * 128 + 128, column:to] = (total * weight).astype(BF16)

        for n in (2, 5):
            rs_copy(i, n).wait_recv()
        half(0, 0, 2)
        if i not in STRAIGHT:
            ag_copy(i, 0).start()
        for n in (3, 4):
            rs_copy(i, n).wait_recv()
        half(1, 3, 1)
        if i in STRAIGHT:
            for z in (2, 1, 3):
                straight_copy(i, z).start()
        else:
            for n in (1, 2, 3):
                ag_copy(i, n).start()

    def forward(i):
        if i not in STRAIGHT:
            ag_copy(i, 0).wait_recv()
            ag_copy(i, 4).start()
            ag_copy(i, 1).wait_recv()
            ag_copy(i, 5).start()

    def a2a_columns(i):
        e, column, width = UNITS[i]
        return e, pl.ds(256 - column - width, width)

    def gradient(i):
        e, column, width = UNITS[i]
        if i in STRAIGHT:
            for z in (1, 3, 2):
                straight_copy(i, z).wait_recv()
        else:
            for n in (2, 3, 4, 5):
                ag_copy(i, n).wait_recv()
        for c in range(column, column + width, 128):
            buf = c_buf if c == 0 else a_buf
            other = gath[e, :, :, c : c + 128].reshape(1024, 128).T
            for w in range(4):
                wide = buf[e, :, :, w * 256 : w * 256 + 256].reshape(1024, 256)
                g = jnp.dot(other, wide, preferred_element_type=F32).T
                grads[e, w * 8 : w * 8 + 8, :, 128 - c : 256 - c] = g.astype(BF16).reshape(8, 32, 128)
        _, k = a2a_columns(i)
        pltpu.make_async_copy(grads.at[e, group, :, k], land.at[e, place, :, k], a2a_recv.at[i]).start()
        for x, y, c in PEERS:
            remote(
                grads.at[e, rank(x, y, c), :, k], land.at[e, place, :, k], a2a_send.at[i], a2a_recv.at[i],
                device(x, y, c),
            ).start()

    def arrive(i):
        e, k = a2a_columns(i)
        pltpu.make_async_copy(land.at[e, :, :, k], land.at[e, :, :, k], a2a_recv.at[i]).wait()
        turned[e % 2, :, :, k] = jnp.swapaxes(land[e, :, :, k].astype(F32), 0, 1).astype(BF16)

    def swap(e):
        return remote(
            contrib.at[e, 1 - core], cross.at[e], cross_send.at[e], cross_recv.at[e], device(0, 0, 1)
        )

    def blocks_ready(_):
        block_load.wait()

    def project(e):
        def half(h):
            def one(n, _):
                o = lax.div(n, 8) * 16 + h * 8 + lax.rem(n, 8)
                contrib[e, h, n] = jnp.dot(turned[e % 2, rows[o]], b_buf[o], preferred_element_type=F32)
                return 0

            lax.fori_loop(0, 32, one, 0, unroll=16)

        half(1 - core)
        swap(e).start()
        half(core)

    def scatter(e):
        swap(e).wait_recv()
        swapped[...] = jnp.swapaxes(contrib[e, core] + cross[e], 0, 1)
        summed[e] = swapped[...].astype(BF16).reshape(CHIPS, 2, 32, 128)
        for k, (x, y) in enumerate(SHIFTS):
            remote(
                summed.at[e, chip_at(x, y)], plane.at[e, k], plane_send.at[e], plane_recv.at[e], device(x, y, 0)
            ).start()
        for k in range(2):
            mine[e, k] = swapped[chip_at(0, 0) * 2 + k]

    def collect(e):
        pltpu.make_async_copy(plane.at[e], plane.at[e], plane_recv.at[e]).wait()
        total = mine[e]
        for k in range(len(SHIFTS)):
            total = total + plane[e, k].astype(F32)
        fsend[e] = total.reshape(2, 4, 8, 128)
        for c in (0, 1):
            for z in range(4):
                src, dst = fsend.at[e, cores[c], z_at[z]], frecv.at[e, core, me]
                if c == 0 and z == 0:
                    pltpu.make_async_copy(src, dst, fin_recv.at[e]).start()
                else:
                    remote(src, dst, fin_send.at[e], fin_recv.at[e], device(0, 0, c, z)).start()

    for copy in small:
        copy.wait()
    far_sums(0)
    near_sums(0)
    pl.semaphore_wait(barrier, len(others))

    order = (
        (low_far, 0), (low_near, 0), (low_far, 1), (low_near, 1), (relay, 0), (low_far, 2), (relay, 1),
        (finish, 0), (finish, 1), (forward, 0), (low_near, 2), (relay, 2), (forward, 1), (low_far, 3),
        (low_far, 4), (gradient, 0), (finish, 2), (low_near, 3), (relay, 3), (gradient, 1), (forward, 2),
        (low_near, 4), (relay, 4), (arrive, 0), (blocks_ready, 0), (project, 0), (low_far, 5), (scatter, 0),
        (finish, 3), (gradient, 2), (low_near, 5), (relay, 5), (arrive, 1), (project, 1), (finish, 4),
        (scatter, 1), (forward, 3), (gradient, 3), (arrive, 2), (forward, 4), (finish, 5), (forward, 5),
        (gradient, 4), (collect, 0), (collect, 1), (gradient, 5), (project, 2), (arrive, 3), (project, 3),
        (scatter, 2), (scatter, 3), (arrive, 4), (arrive, 5), (project, 4), (scatter, 4), (collect, 2),
        (collect, 3), (collect, 4),
    )
    for stage, n in order:
        stage(n)

    for e in range(SEQ):
        pltpu.make_async_copy(frecv.at[e], frecv.at[e], fin_recv.at[e]).wait()
        for h in range(2):
            out[e, h * 8 : h * 8 + 8] = (frecv[e, h, 0] + frecv[e, h, 1]) + (frecv[e, h, 2] + frecv[e, h, 3])

    for i in range(COUNT):
        for n in range(6):
            rs_copy(i, n).wait_send()
        if i in STRAIGHT:
            for z in (1, 2, 3):
                straight_copy(i, z).wait_send()
        else:
            for n in range(6):
                ag_copy(i, n).wait_send()
        e, k = a2a_columns(i)
        sent = land.at[e, pl.ds(0, 31), :, k]
        pltpu.make_async_copy(sent, sent, a2a_send.at[i]).wait()
    for e in range(SEQ):
        swap(e).wait_send()
        for ref, sem in (
            (plane.at[e], plane_send.at[e]),
            (fsend.at[e, 0, pl.ds(0, 3)], fin_send.at[e]),
            (fsend.at[e, 1], fin_send.at[e]),
        ):
            pltpu.make_async_copy(ref, ref, sem).wait()


def local(acts, cotangent, adapter_down, adapter_up, lengths, projection_rows, projection_blocks):
    vmem, hbm = (pl.BlockSpec(memory_space=m) for m in (pltpu.VMEM, pl.ANY))
    dma = pltpu.SemaphoreType.DMA
    out = pl.pallas_call(
        kernel,
        out_shape=jax.ShapeDtypeStruct((SEQ, 16, 128), F32),
        in_specs=[hbm] * 7,
        out_specs=vmem,
        scratch_shapes=[
            pltpu.VMEM((SEQ, 4, 256, 1024), BF16),
            pltpu.VMEM((SEQ, 4, 256, 1024), BF16),
            pltpu.VMEM((64, 256, 128), BF16),
            pltpu.VMEM((1024, 128), BF16),
            pltpu.VMEM((128, 1024), BF16),
            pltpu.SMEM((SEQ,), jnp.int32),
            pltpu.SMEM((64,), jnp.int32),
            pltpu.VMEM((SEQ, 256, 256), F32),
            pltpu.VMEM((SEQ, 2, 128, 256), F32),
            pltpu.VMEM((SEQ, 4, 2, 128, 256), BF16),
            pltpu.VMEM((SEQ, 2, 128, 256), BF16),
            pltpu.VMEM((SEQ, 4, 128, 256), BF16),
            pltpu.VMEM((SEQ, 4, 256, 256), BF16),
            pltpu.VMEM((SEQ, 32, 32, 256), BF16),
            pltpu.VMEM((SEQ, 32, 32, 256), BF16),
            pltpu.VMEM((2, 32, 32, 256), BF16),
            pltpu.VMEM((SEQ, 2, 32, 32, 128), F32),
            pltpu.VMEM((SEQ, 32, 32, 128), F32),
            pltpu.VMEM((32, 32, 128), F32),
            pltpu.VMEM((SEQ, CHIPS, 2, 32, 128), BF16),
            pltpu.VMEM((SEQ, 2, 32, 128), F32),
            pltpu.VMEM((SEQ, CHIPS - 1, 2, 32, 128), BF16),
            pltpu.VMEM((SEQ, 2, 4, 8, 128), F32),
            pltpu.VMEM((SEQ, 2, 4, 8, 128), F32),
            dma((2, SEQ)), dma((4,)), dma, dma((COUNT, 6)), dma((COUNT, 6)), dma((COUNT, 6)), dma((COUNT, 6)), dma((COUNT,)), dma((COUNT,)),
            dma((SEQ,)), dma((SEQ,)), dma((SEQ,)), dma((SEQ,)), dma((SEQ,)), dma((SEQ,)),
        ],
        compiler_params=pltpu.CompilerParams(
            collective_id=0, has_side_effects=True, vmem_limit_bytes=60 * 1024 * 1024
        ),
        cost_estimate=pl.CostEstimate(flops=6 * 10**9, bytes_accessed=25 * 10**6, transcendentals=0),
    )(
        acts.reshape(SEQ, 4, 256, 1024),
        cotangent.reshape(SEQ, 4, 256, 1024),
        adapter_down,
        adapter_up,
        lengths,
        projection_rows.reshape(64),
        projection_blocks.reshape(64, 256, 128),
    )
    return out.reshape(SEQ, 2048)


def solution(mesh):
    placed = (
        P(("dp", "proj"), None, "tensor"),
        P(("dp", "proj"), None, "tensor"),
        P("tensor", None),
        P(None, "tensor"),
        P(("dp", "proj")),
        P("tensor", ("dp", "proj"), None),
        P("tensor", ("dp", "proj"), None, None, None),
    )
    return jax.shard_map(
        local, mesh=mesh, in_specs=placed, out_specs=P(("dp", "proj"), "tensor"), check_vma=False
    )
```

```python
import functools

import jax
import jax.numpy as jnp
from jax import lax
from jax.experimental import pallas as pl
from jax.experimental.pallas import tpu as pltpu
from jax.sharding import PartitionSpec as P

MESH = pl.DeviceIdType.MESH
F32 = jnp.float32
BF16 = jnp.bfloat16
SEQ = 5
UNITS = ((0, 0, 128), (0, 128, 128), (1, 0, 256), (2, 0, 256), (3, 0, 256), (4, 0, 128), (4, 128, 128))
COUNT = len(UNITS)
PARTS = ((0, 0, 32), (1, 0, 32), (2, 0, 32), (3, 0, 32), (4, 0, 16), (4, 16, 16))
STRAIGHT = ()
CHIPS = 16


SHIFTS = (
    (2, 2), (3, 2), (2, 3), (1, 2), (2, 1), (0, 2), (2, 0), (3, 1),
    (1, 3), (3, 3), (1, 1), (0, 3), (3, 0), (0, 1), (1, 0),
)
PEERS = tuple((x, y, c) for x, y in SHIFTS for c in (0, 1)) + ((0, 0, 1),)


def kernel(
    acts, cot, down_in, up_in, lens_in, rows_in, blocks, out,
    a_buf, c_buf, b_buf, down, up, lens, rows, own, relay_f, part, relay_in, fin_in, gath, grads, land, turned,
    contrib, cross, swapped, summed, mine, plane, fsend, frecv,
    load_sem, small_sem, block_sem, rs_send, rs_recv, ag_send, ag_recv, a2a_send, a2a_recv,
    cross_send, cross_recv, plane_send, plane_recv, fin_send, fin_recv,
):
    dp, pj, me = lax.axis_index("dp"), lax.axis_index("proj"), lax.axis_index("tensor")
    group = dp * 2 + pj
    core = lax.rem(dp, 2)
    xx = lax.rem(lax.div(dp, 2), 4)
    yy = lax.div(dp, 8) * 2 + pj
    xs = [lax.rem(xx + d, 4) for d in range(4)]
    ys = [lax.rem(yy + d, 4) for d in range(4)]
    yh = [lax.div(y, 2) for y in ys]
    yl = [lax.rem(y, 2) for y in ys]
    cores = (core, 1 - core)
    z_at = [lax.rem(me + d, 4) for d in range(4)]
    right, far, left = z_at[1:]

    def device(x, y, c, z=0):
        return {"dp": yh[y] * 8 + xs[x] * 2 + cores[c], "proj": yl[y], "tensor": z_at[z]}

    def rank(x, y, c):
        return (yh[y] * 8 + xs[x] * 2 + cores[c]) * 2 + yl[y]

    def chip_at(x, y):
        return (yh[y] * 4 + xs[x]) * 2 + yl[y]

    place = chip_at(0, 0) * 2 + core

    def loads(e):
        return (
            pltpu.make_async_copy(acts.at[e], a_buf.at[e], load_sem.at[0, e]),
            pltpu.make_async_copy(cot.at[e], c_buf.at[e], load_sem.at[1, e]),
        )

    small = [
        pltpu.make_async_copy(src, dst, small_sem.at[n])
        for n, (src, dst) in enumerate(((down_in, down), (up_in, up), (lens_in, lens), (rows_in, rows)))
    ]
    small[0].start()
    loads(0)[0].start()
    small[1].start()
    loads(0)[1].start()
    small[2].start()
    small[3].start()
    block_load = pltpu.make_async_copy(blocks, b_buf, block_sem)

    barrier = pltpu.get_barrier_semaphore()
    others = [device(x, y, c) for x, y, c in PEERS] + [device(0, 0, c, z) for c in (0, 1) for z in (1, 2, 3)]
    for other in others:
        pl.semaphore_signal(barrier, inc=1, device_id=other, device_id_type=MESH)
    for e in range(1, SEQ):
        for copy in loads(e):
            copy.start()
    block_load.start()

    def remote(src, dst, send, recv, to):
        return pltpu.make_async_remote_copy(
            src_ref=src, dst_ref=dst, send_sem=send, recv_sem=recv, device_id=to, device_id_type=MESH
        )

    def rs_copy(i, n):
        e, column, width = UNITS[i]
        q, half, ref, slot, z = (
            (far, 0, relay_in, 1, 3),
            (far, 1, relay_in, 0, 1),
            (right, 0, fin_in, 0, 1),
            (left, 1, fin_in, 3, 3),
            (right, 1, fin_in, 1, 1),
            (left, 0, fin_in, 2, 3),
        )[n]
        columns = pl.ds(column, width)
        return remote(
            part.at[e, q, half, :, columns], ref.at[e, slot, :, columns], rs_send.at[i, n], rs_recv.at[i, n],
            device(0, 0, 0, z),
        )

    def straight_copy(i, z):
        e, column, width = UNITS[i]
        block = gath.at[e, me, :, pl.ds(column, width)]
        return remote(block, block, ag_send.at[i, z - 1], ag_recv.at[i, z - 1], device(0, 0, 0, z))

    def ag_copy(i, n):
        e, column, width = UNITS[i]
        q, half, z = ((me, 0, 1), (me, 1, 3), (me, 1, 1), (me, 0, 3), (left, 0, 1), (right, 1, 3))[n]
        block = gath.at[e, q, pl.ds(half * 128, 128), pl.ds(column, width)]
        return remote(block, block, ag_send.at[i, n], ag_recv.at[i, n], device(0, 0, 0, z))

    def partial(i, q):
        e, column, width = UNITS[i]
        if column == 0:
            yield 0, jnp.dot(a_buf[e, q], down[...], preferred_element_type=F32)
        if column + width == 256:
            yield 128, lax.dot_general(c_buf[e, q], up[...], (((1,), (1,)), ((), ())), preferred_element_type=F32)

    def far_sums(i):
        e, column, width = UNITS[i]
        for side in range(column // 128, (column + width) // 128):
            loads(e)[side].wait()
        for c, value in partial(i, far):
            part[e, far, :, :, c : c + 128] = value.astype(BF16).reshape(2, 128, 128)

    def near_sums(i):
        e = UNITS[i][0]
        for c, value in partial(i, right):
            part[e, right, 0, :, c : c + 128] = value[0:128].astype(BF16)
            relay_f[e, 0, :, c : c + 128] = value[128:256]
        for c, value in partial(i, left):
            part[e, left, 1, :, c : c + 128] = value[128:256].astype(BF16)
            relay_f[e, 1, :, c : c + 128] = value[0:128]

    def low_far(i):
        if i > 1:
            far_sums(i)
        rs_copy(i, 0).start()
        rs_copy(i, 1).start()

    def low_near(i):
        if i > 1:
            near_sums(i)
        rs_copy(i, 2).start()
        rs_copy(i, 3).start()
        for c, value in partial(i, me):
            own[UNITS[i][0], :, c : c + 128] = value

    def relay(i):
        e, column, width = UNITS[i]
        to = column + width
        rs_copy(i, 1).wait_recv()
        part[e, right, 1, :, column:to] = (
            relay_f[e, 0, :, column:to] + relay_in[e, 0, :, column:to].astype(F32)
        ).astype(BF16)
        rs_copy(i, 4).start()
        rs_copy(i, 0).wait_recv()
        part[e, left, 0, :, column:to] = (
            relay_f[e, 1, :, column:to] + relay_in[e, 1, :, column:to].astype(F32)
        ).astype(BF16)
        rs_copy(i, 5).start()

    def finish(i):
        e, column, width = UNITS[i]
        to = column + width
        length = jnp.full((128, width), lens[e], jnp.int32)

        def half(n, first, second):
            token = lax.broadcasted_iota(jnp.int32, (128, width), 0) + (me * 256 + n * 128)
            weight = jnp.where(token < length, 1.0 / length.astype(F32), 0.0)
            total = own[e, n * 128 : n * 128 + 128, column:to] + (
                fin_in[e, first, :, column:to].astype(F32) + fin_in[e, second, :, column:to].astype(F32)
            )
            gath[e, me, n * 128 : n * 128 + 128, column:to] = (total * weight).astype(BF16)

        for n in (2, 5):
            rs_copy(i, n).wait_recv()
        half(0, 0, 2)
        if i not in STRAIGHT:
            ag_copy(i, 0).start()
        for n in (3, 4):
            rs_copy(i, n).wait_recv()
        half(1, 3, 1)
        if i in STRAIGHT:
            for z in (2, 1, 3):
                straight_copy(i, z).start()
        else:
            for n in (1, 2, 3):
                ag_copy(i, n).start()

    def forward(i):
        if i not in STRAIGHT:
            ag_copy(i, 0).wait_recv()
            ag_copy(i, 4).start()
            ag_copy(i, 1).wait_recv()
            ag_copy(i, 5).start()

    def a2a_columns(i):
        e, column, width = UNITS[i]
        return e, pl.ds(256 - column - width, width)

    def gradient(i):
        e, column, width = UNITS[i]
        if i in STRAIGHT:
            for z in (1, 3, 2):
                straight_copy(i, z).wait_recv()
        else:
            for n in (2, 3, 4, 5):
                ag_copy(i, n).wait_recv()
        for c in range(column, column + width, 128):
            buf = c_buf if c == 0 else a_buf
            other = gath[e, :, :, c : c + 128].reshape(1024, 128).T
            for w in range(4):
                wide = buf[e, :, :, w * 256 : w * 256 + 256].reshape(1024, 256)
                g = jnp.dot(other, wide, preferred_element_type=F32).T
                grads[e, w * 8 : w * 8 + 8, :, 128 - c : 256 - c] = g.astype(BF16).reshape(8, 32, 128)
        _, k = a2a_columns(i)
        pltpu.make_async_copy(grads.at[e, group, :, k], land.at[e, place, :, k], a2a_recv.at[i]).start()
        for x, y, c in PEERS:
            remote(
                grads.at[e, rank(x, y, c), :, k], land.at[e, place, :, k], a2a_send.at[i], a2a_recv.at[i],
                device(x, y, c),
            ).start()

    def arrive(i):
        e, k = a2a_columns(i)
        pltpu.make_async_copy(land.at[e, :, :, k], land.at[e, :, :, k], a2a_recv.at[i]).wait()
        turned[e % 2, :, :, k] = jnp.swapaxes(land[e, :, :, k].astype(F32), 0, 1).astype(BF16)

    def swap(p):
        e, first, count = PARTS[p]
        blocks_of = pl.ds(first, count)
        return remote(
            contrib.at[e, 1 - core, blocks_of], cross.at[e, blocks_of], cross_send.at[p], cross_recv.at[p],
            device(0, 0, 1),
        )

    def blocks_ready(_):
        block_load.wait()

    def project(p):
        e, first, count = PARTS[p]

        def half(h):
            def one(n, _):
                o = lax.div(n, 8) * 16 + h * 8 + lax.rem(n, 8)
                contrib[e, h, n] = jnp.dot(turned[e % 2, rows[o]], b_buf[o], preferred_element_type=F32)
                return 0

            lax.fori_loop(first, first + count, one, 0, unroll=16)

        half(1 - core)
        swap(p).start()
        half(core)

    def plane_part(ref, p):
        e, first, count = PARTS[p]
        return ref.at[e, :, :, pl.ds(first, count)]

    def scatter(p):
        e, first, count = PARTS[p]
        last = first + count
        swap(p).wait_recv()
        swapped[:, first:last] = jnp.swapaxes(contrib[e, core, first:last] + cross[e, first:last], 0, 1)
        summed[e, :, :, first:last] = swapped[:, first:last].astype(BF16).reshape(CHIPS, 2, count, 128)
        for k, (x, y) in enumerate(SHIFTS):
            remote(
                summed.at[e, chip_at(x, y), :, pl.ds(first, count)], plane.at[e, k, :, pl.ds(first, count)],
                plane_send.at[p], plane_recv.at[p], device(x, y, 0),
            ).start()
        for k in range(2):
            mine[e, k, first:last] = swapped[chip_at(0, 0) * 2 + k, first:last]

    def collect(e):
        for p, (e_of, _, _) in enumerate(PARTS):
            if e_of == e:
                arrived = plane_part(plane, p)
                pltpu.make_async_copy(arrived, arrived, plane_recv.at[p]).wait()
        total = mine[e]
        for k in range(len(SHIFTS)):
            total = total + plane[e, k].astype(F32)
        fsend[e] = total.reshape(2, 4, 8, 128)
        for c in (0, 1):
            for z in range(4):
                src, dst = fsend.at[e, cores[c], z_at[z]], frecv.at[e, core, me]
                if c == 0 and z == 0:
                    pltpu.make_async_copy(src, dst, fin_recv.at[e]).start()
                else:
                    remote(src, dst, fin_send.at[e], fin_recv.at[e], device(0, 0, c, z)).start()

    for copy in small:
        copy.wait()
    for i in (0, 1):
        far_sums(i)
        near_sums(i)
    pl.semaphore_wait(barrier, len(others))

    order = (
        (low_far, 0), (low_far, 1), (low_far, 2), (low_near, 0), (low_near, 1), (relay, 0), (relay, 1),
        (low_near, 2), (relay, 2), (finish, 0), (finish, 1), (low_far, 3), (forward, 0), (finish, 2),
        (forward, 1), (low_near, 3), (relay, 3), (gradient, 0), (forward, 2), (gradient, 1), (low_far, 4),
        (finish, 3), (gradient, 2), (low_near, 4), (relay, 4), (arrive, 0), (forward, 3), (low_far, 5),
        (low_far, 6), (arrive, 1), (blocks_ready, 0), (project, 0), (low_near, 5), (scatter, 0), (finish, 4),
        (gradient, 3), (low_near, 6), (arrive, 2), (relay, 5), (forward, 4), (relay, 6), (project, 1),
        (scatter, 1), (finish, 5), (gradient, 4), (collect, 0), (finish, 6), (arrive, 3), (forward, 5),
        (project, 2), (forward, 6), (gradient, 5), (gradient, 6), (arrive, 4), (project, 3), (scatter, 2),
        (scatter, 3), (arrive, 5), (collect, 1), (arrive, 6), (project, 4), (project, 5), (scatter, 4),
        (scatter, 5), (collect, 2), (collect, 3), (collect, 4),
    )
    for stage, n in order:
        stage(n)

    for e in range(SEQ):
        pltpu.make_async_copy(frecv.at[e], frecv.at[e], fin_recv.at[e]).wait()
        for h in range(2):
            total = (frecv[e, h, 0] + frecv[e, h, 1]) + (frecv[e, h, 2] + frecv[e, h, 3])
            for n in range(8):
                o = h * 8 + n
                out[e : e + 1, o * 128 : o * 128 + 128] = total[n : n + 1]

    for i in range(COUNT):
        for n in range(6):
            rs_copy(i, n).wait_send()
        if i in STRAIGHT:
            for z in (1, 2, 3):
                straight_copy(i, z).wait_send()
        else:
            for n in range(6):
                ag_copy(i, n).wait_send()
        e, k = a2a_columns(i)
        sent = land.at[e, pl.ds(0, 31), :, k]
        pltpu.make_async_copy(sent, sent, a2a_send.at[i]).wait()
    for p in range(len(PARTS)):
        swap(p).wait_send()
        sent = plane_part(plane, p)
        pltpu.make_async_copy(sent, sent, plane_send.at[p]).wait()
    for e in range(SEQ):
        for ref, sem in (
            (fsend.at[e, 0, pl.ds(0, 3)], fin_send.at[e]),
            (fsend.at[e, 1], fin_send.at[e]),
        ):
            pltpu.make_async_copy(ref, ref, sem).wait()


def local(acts, cotangent, adapter_down, adapter_up, lengths, projection_rows, projection_blocks):
    vmem, hbm = (pl.BlockSpec(memory_space=m) for m in (pltpu.VMEM, pl.ANY))
    dma = pltpu.SemaphoreType.DMA
    return pl.pallas_call(
        kernel,
        out_shape=jax.ShapeDtypeStruct((SEQ, 2048), F32),
        in_specs=[hbm] * 7,
        out_specs=vmem,
        scratch_shapes=[
            pltpu.VMEM((SEQ, 4, 256, 1024), BF16),
            pltpu.VMEM((SEQ, 4, 256, 1024), BF16),
            pltpu.VMEM((64, 256, 128), BF16),
            pltpu.VMEM((1024, 128), BF16),
            pltpu.VMEM((128, 1024), BF16),
            pltpu.SMEM((SEQ,), jnp.int32),
            pltpu.SMEM((64,), jnp.int32),
            pltpu.VMEM((SEQ, 256, 256), F32),
            pltpu.VMEM((SEQ, 2, 128, 256), F32),
            pltpu.VMEM((SEQ, 4, 2, 128, 256), BF16),
            pltpu.VMEM((SEQ, 2, 128, 256), BF16),
            pltpu.VMEM((SEQ, 4, 128, 256), BF16),
            pltpu.VMEM((SEQ, 4, 256, 256), BF16),
            pltpu.VMEM((SEQ, 32, 32, 256), BF16),
            pltpu.VMEM((SEQ, 32, 32, 256), BF16),
            pltpu.VMEM((2, 32, 32, 256), BF16),
            pltpu.VMEM((SEQ, 2, 32, 32, 128), F32),
            pltpu.VMEM((SEQ, 32, 32, 128), F32),
            pltpu.VMEM((32, 32, 128), F32),
            pltpu.VMEM((SEQ, CHIPS, 2, 32, 128), BF16),
            pltpu.VMEM((SEQ, 2, 32, 128), F32),
            pltpu.VMEM((SEQ, CHIPS - 1, 2, 32, 128), BF16),
            pltpu.VMEM((SEQ, 2, 4, 8, 128), F32),
            pltpu.VMEM((SEQ, 2, 4, 8, 128), F32),
            dma((2, SEQ)), dma((4,)), dma, dma((COUNT, 6)), dma((COUNT, 6)), dma((COUNT, 6)), dma((COUNT, 6)), dma((COUNT,)), dma((COUNT,)),
            dma((len(PARTS),)), dma((len(PARTS),)), dma((len(PARTS),)), dma((len(PARTS),)), dma((SEQ,)), dma((SEQ,)),
        ],
        compiler_params=pltpu.CompilerParams(
            collective_id=0, has_side_effects=True, vmem_limit_bytes=60 * 1024 * 1024
        ),
        cost_estimate=pl.CostEstimate(flops=6 * 10**9, bytes_accessed=25 * 10**6, transcendentals=0),
    )(
        acts.reshape(SEQ, 4, 256, 1024),
        cotangent.reshape(SEQ, 4, 256, 1024),
        adapter_down,
        adapter_up,
        lengths,
        projection_rows.reshape(64),
        projection_blocks.reshape(64, 256, 128),
    )


def solution(mesh):
    placed = (
        P(("dp", "proj"), None, "tensor"),
        P(("dp", "proj"), None, "tensor"),
        P("tensor", None),
        P(None, "tensor"),
        P(("dp", "proj")),
        P("tensor", ("dp", "proj"), None),
        P("tensor", ("dp", "proj"), None, None, None),
    )
    return jax.shard_map(
        local, mesh=mesh, in_specs=placed, out_specs=P(("dp", "proj"), "tensor"), check_vma=False
    )
```

```python
import functools

import jax
import jax.numpy as jnp
from jax import lax
from jax.experimental import pallas as pl
from jax.experimental.pallas import tpu as pltpu
from jax.sharding import PartitionSpec as P

MESH = pl.DeviceIdType.MESH
F32 = jnp.float32
BF16 = jnp.bfloat16
SEQ = 5
UNITS = ((0, 0, 128), (0, 128, 128), (1, 0, 256), (2, 0, 256), (3, 0, 256), (4, 0, 128), (4, 128, 128))
COUNT = len(UNITS)
PARTS = ((0, 0, 32), (1, 0, 32), (2, 0, 32), (3, 0, 32), (4, 0, 16), (4, 16, 16))
STRAIGHT = ()
CHIPS = 16


SHIFTS = (
    (2, 2), (3, 2), (2, 3), (1, 2), (2, 1), (0, 2), (2, 0), (3, 1),
    (1, 3), (3, 3), (1, 1), (0, 3), (3, 0), (0, 1), (1, 0),
)
PEERS = tuple((x, y, c) for x, y in SHIFTS for c in (0, 1)) + ((0, 0, 1),)


def kernel(
    acts, cot, down_in, up_in, lens_in, rows_in, blocks, out,
    a_buf, c_buf, b_buf, down, up, lens, rows, own, relay_f, part, relay_in, fin_in, gath, grads, land, turned,
    contrib, cross, swapped, summed, mine, plane, fsend, frecv,
    load_sem, small_sem, block_sem, rs_send, rs_recv, ag_send, ag_recv, a2a_send, a2a_recv,
    cross_send, cross_recv, plane_send, plane_recv, fin_send, fin_recv,
):
    dp, pj, me = lax.axis_index("dp"), lax.axis_index("proj"), lax.axis_index("tensor")
    group = dp * 2 + pj
    core = lax.rem(dp, 2)
    xx = lax.rem(lax.div(dp, 2), 4)
    yy = lax.div(dp, 8) * 2 + pj
    xs = [lax.rem(xx + d, 4) for d in range(4)]
    ys = [lax.rem(yy + d, 4) for d in range(4)]
    yh = [lax.div(y, 2) for y in ys]
    yl = [lax.rem(y, 2) for y in ys]
    cores = (core, 1 - core)
    z_at = [lax.rem(me + d, 4) for d in range(4)]
    right, far, left = z_at[1:]

    def device(x, y, c, z=0):
        return {"dp": yh[y] * 8 + xs[x] * 2 + cores[c], "proj": yl[y], "tensor": z_at[z]}

    def rank(x, y, c):
        return (yh[y] * 8 + xs[x] * 2 + cores[c]) * 2 + yl[y]

    def chip_at(x, y):
        return (yh[y] * 4 + xs[x]) * 2 + yl[y]

    place = chip_at(0, 0) * 2 + core

    def loads(e):
        return (
            pltpu.make_async_copy(acts.at[e], a_buf.at[e], load_sem.at[0, e]),
            pltpu.make_async_copy(cot.at[e], c_buf.at[e], load_sem.at[1, e]),
        )

    small = [
        pltpu.make_async_copy(src, dst, small_sem.at[n])
        for n, (src, dst) in enumerate(((down_in, down), (up_in, up), (lens_in, lens), (rows_in, rows)))
    ]
    small[0].start()
    loads(0)[0].start()
    small[1].start()
    loads(0)[1].start()
    small[2].start()
    small[3].start()
    block_load = pltpu.make_async_copy(blocks, b_buf, block_sem)

    barrier = pltpu.get_barrier_semaphore()
    others = [device(x, y, c) for x, y, c in PEERS] + [device(0, 0, c, z) for c in (0, 1) for z in (1, 2, 3)]
    for other in others:
        pl.semaphore_signal(barrier, inc=1, device_id=other, device_id_type=MESH)
    for e in range(1, SEQ):
        for copy in loads(e):
            copy.start()
    block_load.start()

    def remote(src, dst, send, recv, to):
        return pltpu.make_async_remote_copy(
            src_ref=src, dst_ref=dst, send_sem=send, recv_sem=recv, device_id=to, device_id_type=MESH
        )

    def rs_copy(i, n):
        e, column, width = UNITS[i]
        q, half, ref, slot, z = (
            (far, 0, relay_in, 1, 3),
            (far, 1, relay_in, 0, 1),
            (right, 0, fin_in, 0, 1),
            (left, 1, fin_in, 3, 3),
            (right, 1, fin_in, 1, 1),
            (left, 0, fin_in, 2, 3),
        )[n]
        columns = pl.ds(column, width)
        return remote(
            part.at[e, q, half, :, columns], ref.at[e, slot, :, columns], rs_send.at[i, n], rs_recv.at[i, n],
            device(0, 0, 0, z),
        )

    def straight_copy(i, z):
        e, column, width = UNITS[i]
        block = gath.at[e, me, :, pl.ds(column, width)]
        return remote(block, block, ag_send.at[i, z - 1], ag_recv.at[i, z - 1], device(0, 0, 0, z))

    def ag_copy(i, n):
        e, column, width = UNITS[i]
        q, half, z = ((me, 0, 1), (me, 1, 3), (me, 1, 1), (me, 0, 3), (left, 0, 1), (right, 1, 3))[n]
        block = gath.at[e, q, pl.ds(half * 128, 128), pl.ds(column, width)]
        return remote(block, block, ag_send.at[i, n], ag_recv.at[i, n], device(0, 0, 0, z))

    def partial(i, q):
        e, column, width = UNITS[i]
        if column == 0:
            yield 0, jnp.dot(a_buf[e, q], down[...], preferred_element_type=F32)
        if column + width == 256:
            yield 128, lax.dot_general(c_buf[e, q], up[...], (((1,), (1,)), ((), ())), preferred_element_type=F32)

    def far_sums(i):
        e, column, width = UNITS[i]
        for side in range(column // 128, (column + width) // 128):
            loads(e)[side].wait()
        for c, value in partial(i, far):
            part[e, far, :, :, c : c + 128] = value.astype(BF16).reshape(2, 128, 128)

    def near_sums(i):
        e = UNITS[i][0]
        for c, value in partial(i, right):
            part[e, right, 0, :, c : c + 128] = value[0:128].astype(BF16)
            relay_f[e, 0, :, c : c + 128] = value[128:256]
        for c, value in partial(i, left):
            part[e, left, 1, :, c : c + 128] = value[128:256].astype(BF16)
            relay_f[e, 1, :, c : c + 128] = value[0:128]

    def low_far(i):
        if i:
            far_sums(i)
        rs_copy(i, 0).start()
        rs_copy(i, 1).start()

    def low_near(i):
        if i:
            near_sums(i)
        rs_copy(i, 2).start()
        rs_copy(i, 3).start()
        for c, value in partial(i, me):
            own[UNITS[i][0], :, c : c + 128] = value

    def relay(i):
        e, column, width = UNITS[i]
        to = column + width
        rs_copy(i, 1).wait_recv()
        part[e, right, 1, :, column:to] = (
            relay_f[e, 0, :, column:to] + relay_in[e, 0, :, column:to].astype(F32)
        ).astype(BF16)
        rs_copy(i, 4).start()
        rs_copy(i, 0).wait_recv()
        part[e, left, 0, :, column:to] = (
            relay_f[e, 1, :, column:to] + relay_in[e, 1, :, column:to].astype(F32)
        ).astype(BF16)
        rs_copy(i, 5).start()

    def finish(i):
        e, column, width = UNITS[i]
        to = column + width
        length = jnp.full((128, width), lens[e], jnp.int32)

        def half(n, first, second):
            token = lax.broadcasted_iota(jnp.int32, (128, width), 0) + (me * 256 + n * 128)
            weight = jnp.where(token < length, 1.0 / length.astype(F32), 0.0)
            total = own[e, n * 128 : n * 128 + 128, column:to] + (
                fin_in[e, first, :, column:to].astype(F32) + fin_in[e, second, :, column:to].astype(F32)
            )
            gath[e, me, n * 128 : n * 128 + 128, column:to] = (total * weight).astype(BF16)

        for n in (2, 5):
            rs_copy(i, n).wait_recv()
        half(0, 0, 2)
        if i not in STRAIGHT:
            ag_copy(i, 0).start()
        for n in (3, 4):
            rs_copy(i, n).wait_recv()
        half(1, 3, 1)
        if i in STRAIGHT:
            for z in (2, 1, 3):
                straight_copy(i, z).start()
        else:
            for n in (1, 2, 3):
                ag_copy(i, n).start()

    def forward(i):
        if i not in STRAIGHT:
            ag_copy(i, 0).wait_recv()
            ag_copy(i, 4).start()
            ag_copy(i, 1).wait_recv()
            ag_copy(i, 5).start()

    def a2a_columns(i):
        e, column, width = UNITS[i]
        return e, pl.ds(256 - column - width, width)

    def gradient(i):
        e, column, width = UNITS[i]
        if i in STRAIGHT:
            for z in (1, 3, 2):
                straight_copy(i, z).wait_recv()
        else:
            for n in (2, 3, 4, 5):
                ag_copy(i, n).wait_recv()
        for c in range(column, column + width, 128):
            buf = c_buf if c == 0 else a_buf
            other = gath[e, :, :, c : c + 128].reshape(1024, 128).T
            for w in range(4):
                wide = buf[e, :, :, w * 256 : w * 256 + 256].reshape(1024, 256)
                g = jnp.dot(other, wide, preferred_element_type=F32).T
                grads[e, w * 8 : w * 8 + 8, :, 128 - c : 256 - c] = g.astype(BF16).reshape(8, 32, 128)
        _, k = a2a_columns(i)
        pltpu.make_async_copy(grads.at[e, group, :, k], land.at[e, place, :, k], a2a_recv.at[i]).start()
        for x, y, c in PEERS:
            remote(
                grads.at[e, rank(x, y, c), :, k], land.at[e, place, :, k], a2a_send.at[i], a2a_recv.at[i],
                device(x, y, c),
            ).start()

    def arrive(i):
        e, k = a2a_columns(i)
        pltpu.make_async_copy(land.at[e, :, :, k], land.at[e, :, :, k], a2a_recv.at[i]).wait()
        turned[e % 2, :, :, k] = jnp.swapaxes(land[e, :, :, k].astype(F32), 0, 1).astype(BF16)

    def swap(p):
        e, first, count = PARTS[p]
        blocks_of = pl.ds(first, count)
        return remote(
            contrib.at[e, 1 - core, blocks_of], cross.at[e, blocks_of], cross_send.at[p], cross_recv.at[p],
            device(0, 0, 1),
        )

    def blocks_ready(_):
        block_load.wait()

    def project(p):
        e, first, count = PARTS[p]

        def half(h):
            def one(n, _):
                o = lax.div(n, 8) * 16 + h * 8 + lax.rem(n, 8)
                contrib[e, h, n] = jnp.dot(turned[e % 2, rows[o]], b_buf[o], preferred_element_type=F32)
                return 0

            lax.fori_loop(first, first + count, one, 0, unroll=16)

        half(1 - core)
        swap(p).start()
        half(core)

    def plane_part(ref, p):
        e, first, count = PARTS[p]
        return ref.at[e, :, :, pl.ds(first, count)]

    def scatter(p):
        e, first, count = PARTS[p]
        last = first + count
        swap(p).wait_recv()
        swapped[:, first:last] = jnp.swapaxes(contrib[e, core, first:last] + cross[e, first:last], 0, 1)
        summed[e, :, :, first:last] = swapped[:, first:last].astype(BF16).reshape(CHIPS, 2, count, 128)
        for k, (x, y) in enumerate(SHIFTS):
            remote(
                summed.at[e, chip_at(x, y), :, pl.ds(first, count)], plane.at[e, k, :, pl.ds(first, count)],
                plane_send.at[p], plane_recv.at[p], device(x, y, 0),
            ).start()
        for k in range(2):
            mine[e, k, first:last] = swapped[chip_at(0, 0) * 2 + k, first:last]

    def collect(e):
        for p, (e_of, _, _) in enumerate(PARTS):
            if e_of == e:
                arrived = plane_part(plane, p)
                pltpu.make_async_copy(arrived, arrived, plane_recv.at[p]).wait()
        total = mine[e]
        for k in range(len(SHIFTS)):
            total = total + plane[e, k].astype(F32)
        fsend[e] = total.reshape(2, 4, 8, 128)
        for c in (0, 1):
            for z in range(4):
                src, dst = fsend.at[e, cores[c], z_at[z]], frecv.at[e, core, me]
                if c == 0 and z == 0:
                    pltpu.make_async_copy(src, dst, fin_recv.at[e]).start()
                else:
                    remote(src, dst, fin_send.at[e], fin_recv.at[e], device(0, 0, c, z)).start()

    for copy in small:
        copy.wait()
    far_sums(0)
    near_sums(0)
    pl.semaphore_wait(barrier, len(others))

    order = (
        (low_far, 0), (low_far, 1), (low_far, 2), (low_near, 0), (low_near, 1), (relay, 0), (relay, 1),
        (low_near, 2), (relay, 2), (finish, 0), (finish, 1), (low_far, 3), (forward, 0), (finish, 2),
        (forward, 1), (low_near, 3), (relay, 3), (gradient, 0), (forward, 2), (gradient, 1), (low_far, 4),
        (finish, 3), (gradient, 2), (low_near, 4), (relay, 4), (arrive, 0), (forward, 3), (low_far, 5),
        (low_far, 6), (arrive, 1), (blocks_ready, 0), (project, 0), (low_near, 5), (scatter, 0), (finish, 4),
        (gradient, 3), (low_near, 6), (arrive, 2), (relay, 5), (forward, 4), (relay, 6), (project, 1),
        (scatter, 1), (finish, 5), (gradient, 4), (collect, 0), (finish, 6), (arrive, 3), (forward, 5),
        (project, 2), (forward, 6), (gradient, 5), (gradient, 6), (arrive, 4), (project, 3), (scatter, 2),
        (scatter, 3), (arrive, 5), (collect, 1), (arrive, 6), (project, 4), (project, 5), (scatter, 4),
        (scatter, 5), (collect, 2), (collect, 3), (collect, 4),
    )
    for stage, n in order:
        stage(n)

    for e in range(SEQ):
        pltpu.make_async_copy(frecv.at[e], frecv.at[e], fin_recv.at[e]).wait()
        for h in range(2):
            total = (frecv[e, h, 0] + frecv[e, h, 1]) + (frecv[e, h, 2] + frecv[e, h, 3])
            for n in range(8):
                o = h * 8 + n
                out[e : e + 1, o * 128 : o * 128 + 128] = total[n : n + 1]

    for i in range(COUNT):
        for n in range(6):
            rs_copy(i, n).wait_send()
        if i in STRAIGHT:
            for z in (1, 2, 3):
                straight_copy(i, z).wait_send()
        else:
            for n in range(6):
                ag_copy(i, n).wait_send()
        e, k = a2a_columns(i)
        sent = land.at[e, pl.ds(0, 31), :, k]
        pltpu.make_async_copy(sent, sent, a2a_send.at[i]).wait()
    for p in range(len(PARTS)):
        swap(p).wait_send()
        sent = plane_part(plane, p)
        pltpu.make_async_copy(sent, sent, plane_send.at[p]).wait()
    for e in range(SEQ):
        for ref, sem in (
            (fsend.at[e, 0, pl.ds(0, 3)], fin_send.at[e]),
            (fsend.at[e, 1], fin_send.at[e]),
        ):
            pltpu.make_async_copy(ref, ref, sem).wait()


def local(acts, cotangent, adapter_down, adapter_up, lengths, projection_rows, projection_blocks):
    vmem, hbm = (pl.BlockSpec(memory_space=m) for m in (pltpu.VMEM, pl.ANY))
    dma = pltpu.SemaphoreType.DMA
    return pl.pallas_call(
        kernel,
        out_shape=jax.ShapeDtypeStruct((SEQ, 2048), F32),
        in_specs=[hbm] * 7,
        out_specs=vmem,
        scratch_shapes=[
            pltpu.VMEM((SEQ, 4, 256, 1024), BF16),
            pltpu.VMEM((SEQ, 4, 256, 1024), BF16),
            pltpu.VMEM((64, 256, 128), BF16),
            pltpu.VMEM((1024, 128), BF16),
            pltpu.VMEM((128, 1024), BF16),
            pltpu.SMEM((SEQ,), jnp.int32),
            pltpu.SMEM((64,), jnp.int32),
            pltpu.VMEM((SEQ, 256, 256), F32),
            pltpu.VMEM((SEQ, 2, 128, 256), F32),
            pltpu.VMEM((SEQ, 4, 2, 128, 256), BF16),
            pltpu.VMEM((SEQ, 2, 128, 256), BF16),
            pltpu.VMEM((SEQ, 4, 128, 256), BF16),
            pltpu.VMEM((SEQ, 4, 256, 256), BF16),
            pltpu.VMEM((SEQ, 32, 32, 256), BF16),
            pltpu.VMEM((SEQ, 32, 32, 256), BF16),
            pltpu.VMEM((2, 32, 32, 256), BF16),
            pltpu.VMEM((SEQ, 2, 32, 32, 128), F32),
            pltpu.VMEM((SEQ, 32, 32, 128), F32),
            pltpu.VMEM((32, 32, 128), F32),
            pltpu.VMEM((SEQ, CHIPS, 2, 32, 128), BF16),
            pltpu.VMEM((SEQ, 2, 32, 128), F32),
            pltpu.VMEM((SEQ, CHIPS - 1, 2, 32, 128), BF16),
            pltpu.VMEM((SEQ, 2, 4, 8, 128), F32),
            pltpu.VMEM((SEQ, 2, 4, 8, 128), F32),
            dma((2, SEQ)), dma((4,)), dma, dma((COUNT, 6)), dma((COUNT, 6)), dma((COUNT, 6)), dma((COUNT, 6)), dma((COUNT,)), dma((COUNT,)),
            dma((len(PARTS),)), dma((len(PARTS),)), dma((len(PARTS),)), dma((len(PARTS),)), dma((SEQ,)), dma((SEQ,)),
        ],
        compiler_params=pltpu.CompilerParams(
            collective_id=0, has_side_effects=True, vmem_limit_bytes=60 * 1024 * 1024
        ),
        cost_estimate=pl.CostEstimate(flops=6 * 10**9, bytes_accessed=25 * 10**6, transcendentals=0),
    )(
        acts.reshape(SEQ, 4, 256, 1024),
        cotangent.reshape(SEQ, 4, 256, 1024),
        adapter_down,
        adapter_up,
        lengths,
        projection_rows.reshape(64),
        projection_blocks.reshape(64, 256, 128),
    )


def solution(mesh):
    placed = (
        P(("dp", "proj"), None, "tensor"),
        P(("dp", "proj"), None, "tensor"),
        P("tensor", None),
        P(None, "tensor"),
        P(("dp", "proj")),
        P("tensor", ("dp", "proj"), None),
        P("tensor", ("dp", "proj"), None, None, None),
    )
    return jax.shard_map(
        local, mesh=mesh, in_specs=placed, out_specs=P(("dp", "proj"), "tensor"), check_vma=False
    )
```
